512 devices in a mesh: energy: 16 (over x, y_hi), width: 32 (over z, y_lo, core).
Axes of the slice: x: 4, y: 8 (y_hi: 4, y_lo: 2; y = y_hi * 2 + y_lo), z: 8, core: 2. Of those that a mesh axis runs over, the one named last changes fastest.
Arguments:
- inverse_blocks: bfloat16 [32, 8192, 256], P('energy', 'width')
- source: bfloat16 [32, 8192, 512], P('energy', 'width'), may hold values from -6 to 6
- left_coupling: bfloat16 [1024, 256], P('width'), may hold values from -0.875 to 0.875
- right_coupling: bfloat16 [1024, 256], P('width'), may hold values from -0.875 to 0.875
- energy_weights: float32 [32], P('energy'), may hold values from 0.25 to 2
- collector_low: int32 [32], P('width'), may hold values from 0 to 63
- collector_high: int32 [32], P('width'), may hold values from 193 to 256
Outputs:
- gradient: float32 [32, 256, 256], P('width', 'energy')
The draws below stay inside these ranges and needn't reach their ends.
Inputs may be any that keep to these rules, and one draw needn't show every extreme that they name: collector_low < 64 and collector_high > 192 for every strip.
All inputs are finite; a program needn't handle non-finite values.
Results may differ from the reference program's by a relative error of at most 0.0033.
Values may be sent and summed in bfloat16 or wider, within the bound.
No kernel may reach another device: no remote copies, remote signals or barrier semaphores. Data moves between devices by JAX's collectives and lax.ppermute only.
A program may use at most 64 MiB of HBM per device.

```python
import math
import jax
import jax.numpy as jnp
from jax import lax

B = 256
EDGE = 32
M = 512
SWEEPS = 10
STRIPS = 32
ENERGIES = 32


def draw_inverse_blocks(key, part):
    shape = (ENERGIES, STRIPS * B, B)
    noise = jax.random.normal(key, shape, jnp.float32)
    rows = lax.broadcasted_iota(jnp.int32, shape, 1) % B
    cols = lax.broadcasted_iota(jnp.int32, shape, 2)
    diagonal = jnp.where(rows == cols, 0.6, 0.0)
    return (diagonal + noise * (0.3 / math.sqrt(B))).astype(jnp.bfloat16)


def touch_ends(entries, stream_key, smallest, high):
    longest = entries.shape.index(max(entries.shape))
    spots = []
    for shift in (0, 1):
        where = [jax.random.randint(jax.random.fold_in(stream_key, axis), (), 0, length) for axis, length in enumerate(entries.shape)]
        where[longest] = (where[longest] + shift) % entries.shape[longest]
        spots.append(tuple(where))
    return entries.at[spots[0]].set(smallest).at[spots[1]].set(high)


def levels(rng, extent, pieces, low, largest):
    def one(dim, parts):
        steps = jax.random.uniform(jax.random.fold_in(jax.random.fold_in(rng, 6), dim), (parts,), jnp.float32, low / len(pieces), largest / len(pieces))
        return jnp.repeat(jnp.exp(steps), extent[dim] // parts).reshape((-1,) + (1,) * (len(extent) - dim - 1))

    factor_of = one(*pieces[0])
    for cut in pieces[1:]:
        factor_of = factor_of * one(*cut)
    return factor_of


def scatter_about(rng, dims, spread, bound, split=(), kind=jnp.bfloat16):
    loudness = levels(rng, dims, split, -0.22, 0.18) if split else 1.0
    entries = jax.random.normal(rng, dims, jnp.float32) * spread * loudness
    return jnp.minimum(jnp.maximum(entries, -bound), bound).astype(kind)


def setup_inputs(seed: int = 0) -> dict:
    streams_of = jax.random.split(jax.random.key(seed), 8)
    return {
        "inverse_blocks": draw_inverse_blocks(jax.random.fold_in(streams_of[7], 71), 0),
        "source": scatter_about(streams_of[1], (ENERGIES, STRIPS * B, M), 1.0, 6.0, ((0, 16), (1, 32))),
        "left_coupling": scatter_about(streams_of[2], (STRIPS * EDGE, B), (EDGE + EDGE // 2) ** -0.5, 0.875, ((0, 32),)),
        "right_coupling": scatter_about(streams_of[3], (STRIPS * EDGE, B), (EDGE + EDGE // 2) ** -0.5, 0.875, ((0, 32),)),
        "energy_weights": jnp.clip(jnp.exp(math.log(2.0) - 2.0794415 * jax.random.uniform(streams_of[4], (ENERGIES,), jnp.float32) ** levels(streams_of[4], (ENERGIES,), ((0, 16),), -0.2, 0.2)), 0.25, 2.0),
        "collector_low": touch_ends(jax.random.randint(streams_of[5], (STRIPS,), 0, B // 4), jax.random.fold_in(streams_of[5], 1), 0, (B // 4) - 1).astype(jnp.int32),
        "collector_high": touch_ends(jax.random.randint(streams_of[6], (STRIPS,), 3 * B // 4 + 1, B + 1), jax.random.fold_in(streams_of[6], 1), 3 * B // 4 + 1, B).astype(jnp.int32),
    }


def per_energy(inv_e, src_e, weight, lt32, rt32, mask):
    inv32 = inv_e.astype(jnp.float32)
    src32 = src_e.astype(jnp.float32)
    psi = jnp.einsum('sij,sjm->sim', inv32, src32).astype(jnp.bfloat16)
    for sweep in range(SWEEPS - 1):
        tail = jnp.roll(psi[:, B - EDGE:, :], 1, axis=0).astype(jnp.float32)
        head = jnp.roll(psi[:, :EDGE, :], -1, axis=0).astype(jnp.float32)
        couple = jnp.einsum('sei,sem->sim', lt32, tail) + jnp.einsum('sei,sem->sim', rt32, head)
        rhs = (src32 + couple).astype(jnp.bfloat16).astype(jnp.float32)
        psi = jnp.einsum('sij,sjm->sim', inv32, rhs).astype(jnp.bfloat16)
    psi32 = psi.astype(jnp.float32)
    adjoint_source = 2.0 * weight * mask[:, :, None] * psi32
    lam = jnp.einsum('sji,sjm->sim', inv32, adjoint_source.astype(jnp.bfloat16).astype(jnp.float32)).astype(jnp.bfloat16)
    for sweep in range(SWEEPS - 1):
        lam32 = lam.astype(jnp.float32)
        to_prev = jnp.einsum('sei,sim->sem', lt32, lam32).astype(jnp.bfloat16).astype(jnp.float32)
        to_next = jnp.einsum('sei,sim->sem', rt32, lam32).astype(jnp.bfloat16).astype(jnp.float32)
        from_prev = jnp.roll(to_next, 1, axis=0)
        from_next = jnp.roll(to_prev, -1, axis=0)
        middle = jnp.zeros((STRIPS, B - 2 * EDGE, M), jnp.float32)
        extra = jnp.concatenate([from_prev, middle, from_next], axis=1)
        update = (adjoint_source + extra).astype(jnp.bfloat16).astype(jnp.float32)
        lam = jnp.einsum('sji,sjm->sim', inv32, update).astype(jnp.bfloat16)
    return jnp.einsum('sim,sjm->sij', lam.astype(jnp.float32), psi32)


def reference(inverse_blocks, source, left_coupling, right_coupling, energy_weights, collector_low, collector_high):
    inv = inverse_blocks.reshape(ENERGIES, STRIPS, B, B)
    src = source.reshape(ENERGIES, STRIPS, B, M)
    lt32 = left_coupling.reshape(STRIPS, EDGE, B).astype(jnp.float32)
    rt32 = right_coupling.reshape(STRIPS, EDGE, B).astype(jnp.float32)
    rows = jnp.arange(B, dtype=jnp.int32)
    mask = ((rows[None, :] >= collector_low[:, None]) & (rows[None, :] < collector_high[:, None])).astype(jnp.float32)

    def step(total, items):
        inv_e, src_e, weight = items
        return total + per_energy(inv_e, src_e, weight, lt32, rt32, mask), None

    start = jnp.zeros((STRIPS, B, B), jnp.float32)
    total, unused = lax.scan(step, start, (inv, src, energy_weights))
    return -total / M
```

```python
import jax
import jax.numpy as jnp
from jax import lax
from jax.experimental import pallas as pl
from jax.experimental.pallas import tpu as pltpu
from jax.sharding import PartitionSpec as P

SWEEPS = 10
LANES = 128
F32 = jnp.float32
BF16 = jnp.bfloat16


def mm(a, b):
    return jnp.dot(a, b, preferred_element_type=F32)


def mm_nt(a, b):
    return lax.dot_general(a, b, (((1,), (1,)), ((), ())), preferred_element_type=F32)


def collector_row(low_ref, high_ref, shape, dim):
    at = lax.broadcasted_iota(jnp.int32, shape, dim)
    return (at >= low_ref[0]) & (at < high_ref[0])


def prepare(
    w_ref, low_ref, high_ref, p_hbm, b_hbm, l_hbm, r_hbm, o_ref, p_ref, b_ref, c_ref, sems
):
    count, block, modes = b_ref.shape
    edge = l_hbm.shape[0]
    copies = [
        pltpu.make_async_copy(l_hbm, c_ref.at[pl.ds(0, edge)], sems.at[0]),
        pltpu.make_async_copy(r_hbm, c_ref.at[pl.ds(edge, edge)], sems.at[1]),
        pltpu.make_async_copy(p_hbm, p_ref, sems.at[2]),
        pltpu.make_async_copy(b_hbm, b_ref, sems.at[3]),
    ]
    for copy in copies:
        copy.start()
    for copy in copies[:3]:
        copy.wait()
    couple = c_ref[...]
    inside = collector_row(low_ref, high_ref, (1, block), 1)
    chunk = o_ref.shape[1] - 2 * edge
    each = modes // chunk
    stacks = []
    for e in range(count):
        inverse = p_ref[e]
        rim = jnp.concatenate([inverse[block - edge :], inverse[:edge]], axis=0)
        u = mm_nt(couple, inverse)
        weighted = jnp.where(inside, u * (2.0 * w_ref[e]), 0.0).astype(BF16)
        step = mm_nt(couple, rim)
        middle = mm_nt(weighted, u.astype(BF16))
        exact = jnp.concatenate([step, middle], axis=1)
        outer = mm(weighted, inverse).astype(BF16)
        stacks.append(jnp.concatenate([rim, outer], axis=0))
        left = jnp.zeros_like(exact)
        for k in range(each):
            left += exact
            rounded = left.astype(BF16)
            left -= rounded.astype(F32)
            o_ref[e * each + k, chunk:] = rounded
    copies[3].wait()
    for e in range(count):
        columns = mm(stacks[e], b_ref[e]).T.astype(BF16)
        for k in range(each):
            o_ref[e * each + k, :chunk] = columns[k * chunk : (k + 1) * chunk]


SLOTS = 4


def sweep_all(core_ref, mine_ref, other_ref, o_ref, wf_ref, wa_ref, wk_ref):
    strips, chunk, _ = o_ref.shape
    edge = LANES // SLOTS
    groups = strips // SLOTS
    wide = 2 * LANES
    core = core_ref[0]
    skip = 2 * chunk
    evens, odds = range(0, groups, 2), range(1, groups, 2)

    def strip(s, rows):
        return jnp.where(core == s % 2, mine_ref[s // 2, rows], other_ref[s // 2, rows])

    at = lax.broadcasted_iota(jnp.int32, (1, 2 * wide), 1)
    source = ((at >> 7) << 5) | (at & 31)
    spread = lax.broadcasted_iota(jnp.int32, (LANES, 2 * wide), 0) == source
    spread = spread.astype(F32).astype(BF16)
    at = lax.broadcasted_iota(jnp.int32, (wide, 1), 0)
    source = ((at >> 7) << 5) | (at & 31)
    spread_t = lax.broadcasted_iota(jnp.int32, (wide, LANES), 1) == source
    spread_t = spread_t.astype(F32).astype(BF16)
    row_slot = (lax.broadcasted_iota(jnp.int32, (wide, 1), 0) >> 5) & 3
    lane_slot = (lax.broadcasted_iota(jnp.int32, (1, 2 * wide), 1) >> 5) & 3
    same = row_slot == lane_slot
    for g in range(groups):
        stack = jnp.concatenate(
            [
                strip(g + groups * j, slice(skip + a * edge, skip + (a + 1) * edge))
                for a in range(2)
                for j in range(SLOTS)
            ],
            axis=0,
        )
        both = jnp.where(same, mm(stack, spread), 0.0).astype(BF16)
        wf_ref[g] = both[:, :wide]
        wk_ref[g] = both[:, wide:]
        wa_ref[g] = jnp.where(same[:, :wide], mm_nt(spread_t, stack), 0.0).astype(BF16)

    at = lax.broadcasted_iota(jnp.int32, (1, 2 * wide), 1)
    source = (((at >> 5) & 3) << 7) | ((at >> 7) << 5) | (at & 31)
    order = lax.broadcasted_iota(jnp.int32, (2 * wide, 2 * wide), 0) == source
    order = order.astype(F32).astype(BF16)
    mine = pl.ds(pl.multiple_of(core * chunk, chunk), chunk)
    start = jnp.concatenate(
        [
            jnp.concatenate([strip(g + groups * j, mine) for j in range(SLOTS)], axis=1)
            for g in range(groups)
        ],
        axis=0,
    )
    start = mm(start, order)

    def up(parts, at):
        if at == 1:
            return [pltpu.roll(parts[-1], edge, 1)] + parts[:-1]
        return list(parts)

    def down(parts, at):
        if at == 1:
            return list(parts)
        return parts[1:] + [pltpu.roll(parts[0], LANES - edge, 1)]

    def arrive(parts, at, first_up):
        first, second = [v[:, :LANES] for v in parts], [v[:, LANES:] for v in parts]
        if first_up:
            first, second = up(first, at), down(second, at)
        else:
            first, second = down(first, at), up(second, at)
        return [jnp.concatenate([p, q], axis=1).astype(BF16) for p, q in zip(first, second)]

    def iterate(base, weights, first_up):
        even, odd = [base[g] for g in evens], [base[g] for g in odds]
        ahead, behind = odd, even
        z = arrive(ahead, 1, first_up)
        ahead = [even[i] + mm(z[i], weights[g]) for i, g in enumerate(evens)]
        for t in range(1, SWEEPS - 2):
            at = (t + 1) % 2
            z = arrive(ahead, at, first_up)
            y = arrive(behind, at, first_up)
            add = odd if at == 0 else even
            both = []
            for i, g in enumerate(odds if at == 0 else evens):
                both.append(mm(jnp.concatenate([z[i], y[i]], axis=0), weights[g]))
            ahead = [add[i] + v[:chunk] for i, v in enumerate(both)]
            behind = [add[i] + v[chunk:] for i, v in enumerate(both)]
        at = (SWEEPS - 1) % 2
        y = arrive(behind, at, first_up)
        add = odd if at == 0 else even
        behind = [
            add[i] + mm(y[i], weights[g]) for i, g in enumerate(odds if at == 0 else evens)
        ]
        gets_ahead, gets_behind = arrive(ahead, at, first_up), arrive(behind, 1 - at, first_up)
        got = [None] * groups
        for i, g in enumerate(odds if at == 0 else evens):
            got[g] = gets_ahead[i]
        for i, g in enumerate(evens if at == 0 else odds):
            got[g] = gets_behind[i]
        return got

    base = [start[g * chunk : (g + 1) * chunk, :wide] for g in range(groups)]
    z = iterate(base, wf_ref, True)
    base = [
        start[g * chunk : (g + 1) * chunk, wide:] + mm(z[g], wk_ref[g]) for g in range(groups)
    ]
    y = iterate(base, wa_ref, False)
    out = jnp.concatenate(
        [jnp.concatenate([z[g], y[g]], axis=1) for g in range(groups)], axis=0
    )
    out = mm(out, order).astype(BF16)
    for g in range(groups):
        for j in range(SLOTS):
            o_ref[g + groups * j] = out[g * chunk : (g + 1) * chunk, j * LANES : (j + 1) * LANES]


def finish(w_ref, low_ref, high_ref, p_ref, b_ref, l_ref, r_ref, zy_ref, o_ref):
    count, block, modes = b_ref.shape
    edge = l_ref.shape[0]
    couple = jnp.concatenate([l_ref[...], r_ref[...]], axis=0).astype(F32).T.astype(BF16)
    couple = jnp.concatenate([couple, jnp.zeros_like(couple)], axis=1)
    inside = collector_row(low_ref, high_ref, (block, 1), 0)
    pick = (
        lax.broadcasted_iota(jnp.int32, (2 * edge, LANES), 0) + 2 * edge
        == lax.broadcasted_iota(jnp.int32, (2 * edge, LANES), 1)
    ).astype(F32).astype(BF16)
    total = jnp.zeros((block, block), F32)
    for e in range(count):
        inverse = p_ref[e]
        got = mm_nt(jnp.concatenate([couple, pick], axis=0), zy_ref[e])
        rhs = (b_ref[e].astype(F32) + got[:block]).astype(BF16)
        psi = mm(inverse, rhs).astype(BF16)
        source = jnp.where(inside, psi.astype(F32) * (2.0 * w_ref[e]), 0.0)
        update = jnp.concatenate(
            [
                source[:edge] + got[block + edge :],
                source[edge : block - edge],
                source[block - edge :] + got[block : block + edge],
            ],
            axis=0,
        ).astype(BF16)
        lam = lax.dot_general(
            inverse, update, (((0,), (0,)), ((), ())), preferred_element_type=F32
        ).astype(BF16)
        total += mm_nt(lam, psi)
    total = (total * (-1.0 / modes)).astype(BF16)
    pieces, owned, _ = o_ref.shape
    for k in range(pieces):
        o_ref[k] = total[k * owned : (k + 1) * owned]


SMEM = pl.BlockSpec(memory_space=pltpu.SMEM)
VMEM = pl.BlockSpec(memory_space=pltpu.VMEM)
ANY = pl.BlockSpec(memory_space=pltpu.HBM)
PARAMS = dict(compiler_params=pltpu.CompilerParams(vmem_limit_bytes=24 * 1024 * 1024))


def body(
    inverse_blocks,
    source,
    left_coupling,
    right_coupling,
    energy_weights,
    collector_low,
    collector_high,
):
    count, block, modes = source.shape
    edge = left_coupling.shape[0]
    chips = lax.axis_size("chip")
    cores = lax.axis_size("core")
    strips = chips * cores
    energies = lax.axis_size("energy")
    chunk = count * modes // strips
    owned = block // energies
    scalars = (energy_weights, collector_low, collector_high)
    shape = jax.ShapeDtypeStruct

    pieces = pl.pallas_call(
        prepare,
        out_shape=shape((chips, cores * chunk + 2 * edge, 4 * edge), BF16),
        in_specs=[SMEM] * 3 + [ANY] * 4,
        out_specs=VMEM,
        scratch_shapes=[
            pltpu.VMEM((count, block, block), BF16),
            pltpu.VMEM((count, block, modes), BF16),
            pltpu.VMEM((2 * edge, block), BF16),
            pltpu.SemaphoreType.DMA((4,)),
        ],
        name="prepare",
    )(*scalars, inverse_blocks, source, left_coupling, right_coupling)
    mine = lax.all_to_all(pieces, "chip", 0, 0, tiled=True)
    other = lax.ppermute(mine, "core", [(i, cores - 1 - i) for i in range(cores)])
    core = lax.axis_index("core").astype(jnp.int32).reshape(1)
    weights = pltpu.VMEM((strips // SLOTS, 2 * LANES, 2 * LANES), BF16)
    out = pl.pallas_call(
        sweep_all,
        out_shape=shape((strips, chunk, 4 * edge), BF16),
        in_specs=[SMEM] + [VMEM] * 2,
        out_specs=VMEM,
        scratch_shapes=[weights] * 3,
        name="sweeps",
        **PARAMS,
    )(core, mine, other)
    out = lax.all_to_all(out, ("chip", "core"), 0, 0, tiled=True)
    out = pl.pallas_call(
        finish,
        out_shape=shape((energies, owned, block), BF16),
        in_specs=[SMEM] * 3 + [VMEM] * 5,
        out_specs=VMEM,
        name="finish",
        **PARAMS,
    )(
        *scalars,
        inverse_blocks,
        source,
        left_coupling,
        right_coupling,
        out.reshape(count, modes, 4 * edge),
    )
    out = lax.all_to_all(out, "energy", 0, 0, tiled=True)
    return jnp.sum(out.astype(F32), axis=0)[None]


def solution(mesh):
    energies, strips = mesh.devices.shape
    cores = 2
    split = jax.sharding.Mesh(
        mesh.devices.reshape(energies, strips // cores, cores), ("energy", "chip", "core")
    )
    width = ("chip", "core")
    placed = (
        P("energy", width, None),
        P("energy", width, None),
        P(width, None),
        P(width, None),
        P("energy"),
        P(width),
        P(width),
    )
    return jax.shard_map(
        body, mesh=split, in_specs=placed, out_specs=P(width, "energy", None), check_vma=False
    )
```

```python
import jax
import jax.numpy as jnp
from jax import lax
from jax.experimental import pallas as pl
from jax.experimental.pallas import tpu as pltpu
from jax.sharding import PartitionSpec as P

SWEEPS = 10
LANES = 128
F32 = jnp.float32
BF16 = jnp.bfloat16


def mm(a, b):
    return jnp.dot(a, b, preferred_element_type=F32)


def mm_nt(a, b):
    return lax.dot_general(a, b, (((1,), (1,)), ((), ())), preferred_element_type=F32)


def prepare(
    w_hbm,
    low_hbm,
    high_hbm,
    p_hbm,
    b_hbm,
    l_hbm,
    r_hbm,
    o_hbm,
    scale_hbm,
    w_ref,
    low_ref,
    high_ref,
    p_ref,
    b_ref,
    c_ref,
    o_ref,
    scale_ref,
    sems,
):
    count, block, modes = b_ref.shape
    edge = l_hbm.shape[0]
    fetch = [
        (w_hbm, w_ref),
        (low_hbm, low_ref),
        (high_hbm, high_ref),
        (l_hbm, c_ref.at[pl.ds(0, edge)]),
        (r_hbm, c_ref.at[pl.ds(edge, edge)]),
        (p_hbm, p_ref),
        (b_hbm, b_ref),
    ]
    fetch = [pltpu.make_async_copy(*ends, sems.at[i]) for i, ends in enumerate(fetch)]
    for copy in fetch:
        copy.start()
    for copy in fetch[:3]:
        copy.wait()
    low, high = low_ref[0], high_ref[0]
    at = lax.broadcasted_iota(jnp.int32, (block, LANES), 0)
    inside = (at >= low) & (at < high)
    for e in range(count):
        scale_ref[e] = jnp.where(inside, 2.0 * w_ref[e], 0.0)
    keep = [pltpu.make_async_copy(scale_ref, scale_hbm, sems.at[len(fetch)])]
    keep[0].start()
    at = lax.broadcasted_iota(jnp.int32, (1, block), 1)
    inside = (at >= low) & (at < high)
    for copy in fetch[3:6]:
        copy.wait()
    couple = c_ref[...]
    chunk = o_ref.shape[1] - 2 * edge
    each = modes // chunk
    energies = range(count)
    rim = [jnp.concatenate([p_ref[e, block - edge :], p_ref[e, :edge]], axis=0) for e in energies]
    u = [mm_nt(couple, p_ref[e]) for e in energies]
    step = [mm_nt(couple, rim[e]) for e in energies]
    weighted = [jnp.where(inside, u[e] * (2.0 * w_ref[e]), 0.0).astype(BF16) for e in energies]
    outer = [mm(weighted[e], p_ref[e]).astype(BF16) for e in energies]
    middle = [mm_nt(weighted[e], u[e].astype(BF16)) for e in energies]
    fetch[6].wait()
    for e in energies:
        rows = mm(jnp.concatenate([rim[e], outer[e]], axis=0), b_ref[e])
        columns = rows.T.astype(BF16)
        exact = jnp.concatenate([step[e], middle[e]], axis=1)
        left = jnp.zeros_like(exact)
        for k in range(each):
            left += exact
            rounded = left.astype(BF16)
            left -= rounded.astype(F32)
            o_ref[e * each + k, chunk:] = rounded
            o_ref[e * each + k, :chunk] = columns[k * chunk : (k + 1) * chunk]
        part = pl.ds(e * each, each)
        keep.append(
            pltpu.make_async_copy(o_ref.at[part], o_hbm.at[part], sems.at[len(fetch) + 1 + e])
        )
        keep[-1].start()
    for copy in keep:
        copy.wait()


SLOTS = 4


def sweep_all(core_ref, mine_ref, other_ref, o_ref, wf_ref, wa_ref, wk_ref):
    strips, chunk, _ = o_ref.shape
    edge = LANES // SLOTS
    groups = strips // SLOTS
    wide = 2 * LANES
    core = core_ref[0]
    skip = 2 * chunk
    evens, odds = range(0, groups, 2), range(1, groups, 2)

    def strip(s, rows):
        return jnp.where(core == s % 2, mine_ref[s // 2, rows], other_ref[s // 2, rows])

    at = lax.broadcasted_iota(jnp.int32, (1, 2 * wide), 1)
    source = ((at >> 7) << 5) | (at & 31)
    spread = lax.broadcasted_iota(jnp.int32, (LANES, 2 * wide), 0) == source
    spread = spread.astype(F32).astype(BF16)
    at = lax.broadcasted_iota(jnp.int32, (wide, 1), 0)
    source = ((at >> 7) << 5) | (at & 31)
    spread_t = lax.broadcasted_iota(jnp.int32, (wide, LANES), 1) == source
    spread_t = spread_t.astype(F32).astype(BF16)
    row_slot = (lax.broadcasted_iota(jnp.int32, (wide, 1), 0) >> 5) & 3
    lane_slot = (lax.broadcasted_iota(jnp.int32, (1, 2 * wide), 1) >> 5) & 3
    def stacked(g, turns):
        return jnp.concatenate(
            [
                strip(
                    g + groups * ((j + turns[a]) % SLOTS),
                    slice(skip + a * edge, skip + (a + 1) * edge),
                )
                for a in range(2)
                for j in range(SLOTS)
            ],
            axis=0,
        )

    def matching(turns, lanes):
        half = lax.broadcasted_iota(jnp.int32, (wide, 1), 0) >> 7
        slot = row_slot + jnp.where(half == 0, turns[0], turns[1])
        return (slot & 3) == lane_slot[:, :lanes]

    last = groups - 1
    for g in range(groups):
        turns = {0: (1, 0), last: (0, -1)}.get(g, (0, 0))
        back = {0: (0, 1), last: (-1, 0)}.get(g, (0, 0))
        both = mm(stacked(g, turns), spread)
        both = jnp.where(matching(turns, 2 * wide), both, 0.0).astype(BF16)
        wf_ref[g] = both[:, :wide]
        wk_ref[g] = both[:, wide:]
        both = mm_nt(spread_t, stacked(g, (0, 0)))
        wa_ref[g] = jnp.where(matching(back, wide), both, 0.0).astype(BF16)

    at = lax.broadcasted_iota(jnp.int32, (1, 2 * wide), 1)
    source = (((at >> 5) & 3) << 7) | ((at >> 7) << 5) | (at & 31)
    order = lax.broadcasted_iota(jnp.int32, (2 * wide, 2 * wide), 0) == source
    order = order.astype(F32).astype(BF16)
    mine = pl.ds(pl.multiple_of(core * chunk, chunk), chunk)
    start = jnp.concatenate(
        [
            jnp.concatenate([strip(g + groups * j, mine) for j in range(SLOTS)], axis=1)
            for g in range(groups)
        ],
        axis=0,
    )
    start = mm(start, order)

    def up(parts, at):
        return [parts[-1]] + parts[:-1] if at == 1 else list(parts)

    def down(parts, at):
        return list(parts) if at == 1 else parts[1:] + [parts[0]]

    def arrive(parts, at, first_up):
        first, second = [v[:, :LANES] for v in parts], [v[:, LANES:] for v in parts]
        if first_up:
            first, second = up(first, at), down(second, at)
        else:
            first, second = down(first, at), up(second, at)
        return [jnp.concatenate([p, q], axis=1).astype(BF16) for p, q in zip(first, second)]

    def turned(parts, first_up):
        def turn(part, half, by):
            halves = [part[:, :LANES], part[:, LANES:]]
            halves[half] = pltpu.roll(halves[half].astype(F32), by, 1).astype(BF16)
            return jnp.concatenate(halves, axis=1)

        parts = list(parts)
        parts[0] = turn(parts[0], 0 if first_up else 1, edge)
        parts[last] = turn(parts[last], 1 if first_up else 0, LANES - edge)
        return parts

    def iterate(base, weights, first_up):
        even, odd = [base[g] for g in evens], [base[g] for g in odds]
        ahead, behind = odd, even
        z = arrive(ahead, 1, first_up)
        ahead = [even[i] + mm(z[i], weights[g]) for i, g in enumerate(evens)]
        for t in range(1, SWEEPS - 2):
            at = (t + 1) % 2
            z = arrive(ahead, at, first_up)
            y = arrive(behind, at, first_up)
            add = odd if at == 0 else even
            both = []
            for i, g in enumerate(odds if at == 0 else evens):
                both.append(mm(jnp.concatenate([z[i], y[i]], axis=0), weights[g]))
            ahead = [add[i] + v[:chunk] for i, v in enumerate(both)]
            behind = [add[i] + v[chunk:] for i, v in enumerate(both)]
        at = (SWEEPS - 1) % 2
        y = arrive(behind, at, first_up)
        add = odd if at == 0 else even
        behind = [
            add[i] + mm(y[i], weights[g]) for i, g in enumerate(odds if at == 0 else evens)
        ]
        gets_ahead, gets_behind = arrive(ahead, at, first_up), arrive(behind, 1 - at, first_up)
        got = [None] * groups
        for i, g in enumerate(odds if at == 0 else evens):
            got[g] = gets_ahead[i]
        for i, g in enumerate(evens if at == 0 else odds):
            got[g] = gets_behind[i]
        return got

    base = [start[g * chunk : (g + 1) * chunk, :wide] for g in range(groups)]
    z = iterate(base, wf_ref, True)
    base = [
        start[g * chunk : (g + 1) * chunk, wide:] + mm(z[g], wk_ref[g]) for g in range(groups)
    ]
    y = iterate(base, wa_ref, False)
    z, y = turned(z, True), turned(y, False)
    out = jnp.concatenate(
        [jnp.concatenate([z[g], y[g]], axis=1) for g in range(groups)], axis=0
    )
    out = mm(out, order).astype(BF16)
    for g in range(groups):
        for j in range(SLOTS):
            o_ref[g + groups * j] = out[g * chunk : (g + 1) * chunk, j * LANES : (j + 1) * LANES]


def finish(scale_ref, p_ref, b_ref, l_ref, r_ref, zy_ref, o_ref):
    count, block, modes = b_ref.shape
    edge = l_ref.shape[0]
    couple = jnp.concatenate([l_ref[...], r_ref[...]], axis=0).astype(F32).T.astype(BF16)
    couple = jnp.concatenate([couple, jnp.zeros_like(couple)], axis=1)
    pick = (
        lax.broadcasted_iota(jnp.int32, (2 * edge, LANES), 0) + 2 * edge
        == lax.broadcasted_iota(jnp.int32, (2 * edge, LANES), 1)
    ).astype(F32).astype(BF16)
    front = jnp.concatenate([couple, pick], axis=0)
    energies = range(count)
    got = [mm_nt(front, zy_ref[e]) for e in energies]
    rhs = [(b_ref[e].astype(F32) + got[e][:block]).astype(BF16) for e in energies]
    psi = [mm(p_ref[e], rhs[e]).astype(BF16) for e in energies]
    scale = [jnp.concatenate([scale_ref[e]] * (modes // LANES), axis=1) for e in energies]
    source = [psi[e].astype(F32) * scale[e] for e in energies]
    update = [
        jnp.concatenate(
            [
                source[e][:edge] + got[e][block + edge :],
                source[e][edge : block - edge],
                source[e][block - edge :] + got[e][block : block + edge],
            ],
            axis=0,
        ).astype(BF16)
        for e in energies
    ]
    total = jnp.zeros((block, block), F32)
    for e in energies:
        part = mm_nt(update[e], psi[e])
        high = part.astype(BF16)
        low = (part - high.astype(F32)).astype(BF16)
        inverse_t = p_ref[e].T
        total += mm(inverse_t, high) + mm(inverse_t, low)
    total = (total * (-1.0 / modes)).astype(BF16)
    pieces, owned, _ = o_ref.shape
    for k in range(pieces):
        o_ref[k] = total[k * owned : (k + 1) * owned]


SMEM = pl.BlockSpec(memory_space=pltpu.SMEM)
VMEM = pl.BlockSpec(memory_space=pltpu.VMEM)
ANY = pl.BlockSpec(memory_space=pltpu.HBM)
PARAMS = dict(compiler_params=pltpu.CompilerParams(vmem_limit_bytes=24 * 1024 * 1024))


shape = jax.ShapeDtypeStruct


def call_prepare(scalars, inverse, source, left, right, chips, cores, chunk):
    count, block, modes = source.shape
    edge = left.shape[0]
    pieces = (chips, cores * chunk + 2 * edge, 4 * edge)
    return pl.pallas_call(
        prepare,
        out_shape=(shape(pieces, BF16), shape((count, block, LANES), F32)),
        in_specs=[ANY] * 7,
        out_specs=(ANY, ANY),
        scratch_shapes=[
            pltpu.SMEM((count,), F32),
            pltpu.SMEM((1,), jnp.int32),
            pltpu.SMEM((1,), jnp.int32),
            pltpu.VMEM((count, block, block), BF16),
            pltpu.VMEM((count, block, modes), BF16),
            pltpu.VMEM((2 * edge, block), BF16),
            pltpu.VMEM(pieces, BF16),
            pltpu.VMEM((count, block, LANES), F32),
            pltpu.SemaphoreType.DMA((8 + count,)),
        ],
        name="prepare",
    )(*scalars, inverse, source, left, right)


def call_sweeps(core, mine, other):
    chips, rows, lanes = mine.shape
    strips = 2 * chips
    chunk = (rows - 2 * lanes // SLOTS) // 2
    weights = pltpu.VMEM((strips // SLOTS, 2 * LANES, 2 * LANES), BF16)
    return pl.pallas_call(
        sweep_all,
        out_shape=shape((strips, chunk, lanes), BF16),
        in_specs=[SMEM] + [VMEM] * 2,
        out_specs=VMEM,
        scratch_shapes=[weights] * 3,
        name="sweeps",
        **PARAMS,
    )(core, mine, other)


def call_finish(scale, inverse, source, left, right, columns, energies, owned):
    block = inverse.shape[1]
    return pl.pallas_call(
        finish,
        out_shape=shape((energies, owned, block), BF16),
        in_specs=[VMEM] * 6,
        out_specs=VMEM,
        name="finish",
        **PARAMS,
    )(scale, inverse, source, left, right, columns)


def body(
    inverse_blocks,
    source,
    left_coupling,
    right_coupling,
    energy_weights,
    collector_low,
    collector_high,
):
    count, block, modes = source.shape
    edge = left_coupling.shape[0]
    chips = lax.axis_size("chip")
    cores = lax.axis_size("core")
    strips = chips * cores
    energies = lax.axis_size("energy")
    chunk = count * modes // strips
    owned = block // energies
    scalars = (energy_weights, collector_low, collector_high)

    pieces, scale = call_prepare(
        scalars, inverse_blocks, source, left_coupling, right_coupling, chips, cores, chunk
    )
    mine = lax.all_to_all(pieces, "chip", 0, 0, tiled=True)
    other = lax.ppermute(mine, "core", [(i, cores - 1 - i) for i in range(cores)])
    core = lax.axis_index("core").astype(jnp.int32).reshape(1)
    out = call_sweeps(core, mine, other)
    out = lax.all_to_all(out, ("chip", "core"), 0, 0, tiled=True)
    out = call_finish(
        scale,
        inverse_blocks,
        source,
        left_coupling,
        right_coupling,
        out.reshape(count, modes, 4 * edge),
        energies,
        owned,
    )
    out = lax.all_to_all(out, "energy", 0, 0, tiled=True)
    return jnp.sum(out.astype(F32), axis=0)[None]


def solution(mesh):
    energies, strips = mesh.devices.shape
    cores = 2
    split = jax.sharding.Mesh(
        mesh.devices.reshape(energies, strips // cores, cores), ("energy", "chip", "core")
    )
    width = ("chip", "core")
    placed = (
        P("energy", width, None),
        P("energy", width, None),
        P(width, None),
        P(width, None),
        P("energy"),
        P(width),
        P(width),
    )
    return jax.shard_map(
        body, mesh=split, in_specs=placed, out_specs=P(width, "energy", None), check_vma=False
    )
```

```python
import jax
import jax.numpy as jnp
from jax import lax
from jax.experimental import pallas as pl
from jax.experimental.pallas import tpu as pltpu
from jax.sharding import PartitionSpec as P

SWEEPS = 10
LANES = 128
F32 = jnp.float32
BF16 = jnp.bfloat16


def mm(a, b):
    return jnp.dot(a, b, preferred_element_type=F32)


def mm_nt(a, b):
    return lax.dot_general(a, b, (((1,), (1,)), ((), ())), preferred_element_type=F32)


def pack(step, middle):
    edge = step.shape[0] // 2
    most = edge * 3 // 4
    low = [step[edge:, :edge], step[edge:, edge:], middle[edge:, edge:]]
    rest = jnp.concatenate([v[most:] for v in low], axis=0)
    return jnp.concatenate(
        [
            jnp.concatenate([step[:edge], middle[:edge]], axis=1),
            jnp.concatenate([v[:most] for v in low] + [rest], axis=1),
        ],
        axis=0,
    )


def prepare(
    w_hbm,
    low_hbm,
    high_hbm,
    p_hbm,
    b_hbm,
    l_hbm,
    r_hbm,
    o_hbm,
    scale_hbm,
    w_ref,
    low_ref,
    high_ref,
    p_ref,
    b_ref,
    c_ref,
    o_ref,
    scale_ref,
    sems,
):
    count, block, modes = b_ref.shape
    edge = l_hbm.shape[0]
    fetch = [
        (w_hbm, w_ref),
        (low_hbm, low_ref),
        (high_hbm, high_ref),
        (l_hbm, c_ref.at[pl.ds(0, edge)]),
        (r_hbm, c_ref.at[pl.ds(edge, edge)]),
        (p_hbm, p_ref),
        (b_hbm, b_ref),
    ]
    fetch = [pltpu.make_async_copy(*ends, sems.at[i]) for i, ends in enumerate(fetch)]
    for copy in fetch:
        copy.start()
    for copy in fetch[:3]:
        copy.wait()
    low, high = low_ref[0], high_ref[0]
    at = lax.broadcasted_iota(jnp.int32, (block, LANES), 0)
    inside = (at >= low) & (at < high)
    for e in range(count):
        scale_ref[e] = jnp.where(inside, 2.0 * w_ref[e], 0.0)
    keep = [pltpu.make_async_copy(scale_ref, scale_hbm, sems.at[len(fetch)])]
    keep[0].start()
    at = lax.broadcasted_iota(jnp.int32, (1, block), 1)
    inside = (at >= low) & (at < high)
    for copy in fetch[3:6]:
        copy.wait()
    couple = c_ref[...]
    each = o_ref.shape[0] // count
    chunk = modes // each
    energies = range(count)
    rim = [jnp.concatenate([p_ref[e, block - edge :], p_ref[e, :edge]], axis=0) for e in energies]
    u = [mm_nt(couple, p_ref[e]) for e in energies]
    step = [mm_nt(couple, rim[e]) for e in energies]
    weighted = [jnp.where(inside, u[e] * (2.0 * w_ref[e]), 0.0).astype(BF16) for e in energies]
    outer = [mm(weighted[e], p_ref[e]).astype(BF16) for e in energies]
    middle = [mm_nt(weighted[e], u[e].astype(BF16)) for e in energies]
    fetch[6].wait()
    for e in energies:
        rows = mm(jnp.concatenate([rim[e], outer[e]], axis=0), b_ref[e])
        columns = rows.T.astype(BF16)
        exact = pack(step[e], middle[e])
        left = jnp.zeros_like(exact)
        for k in range(each):
            left += exact
            rounded = left.astype(BF16)
            left -= rounded.astype(F32)
            o_ref[e * each + k, chunk:] = rounded
            o_ref[e * each + k, :chunk] = columns[k * chunk : (k + 1) * chunk]
        part = pl.ds(e * each, each)
        keep.append(
            pltpu.make_async_copy(o_ref.at[part], o_hbm.at[part], sems.at[len(fetch) + 1 + e])
        )
        keep[-1].start()
    for copy in keep:
        copy.wait()


SLOTS = 4


def sweep_all(core_ref, x_ref, o_ref, wf_ref, wa_ref, wk_ref):
    strips, chunk, _ = o_ref.shape
    edge = LANES // SLOTS
    most = edge * 3 // 4
    groups = strips // SLOTS
    wide = 2 * LANES
    last = groups - 1
    core = core_ref[0]
    skip = x_ref.shape[0] * chunk
    evens, odds = range(0, groups, 2), range(1, groups, 2)

    def strip(s, rows):
        return x_ref[s % 2, s // 2, rows]

    at = lax.broadcasted_iota(jnp.int32, (1, 2 * wide), 1)
    source = ((at >> 7) << 5) | (at & 31)
    spread = lax.broadcasted_iota(jnp.int32, (LANES, 2 * wide), 0) == source
    spread = spread.astype(F32).astype(BF16)
    source = (lax.broadcasted_iota(jnp.int32, (LANES, 1), 0) & 31) | 96
    spread_t = lax.broadcasted_iota(jnp.int32, (LANES, LANES), 1) == source
    spread_t = spread_t.astype(F32).astype(BF16)
    row_slot = lax.broadcasted_iota(jnp.int32, (LANES, 1), 0) >> 5
    lane_slot = (lax.broadcasted_iota(jnp.int32, (1, wide), 1) >> 5) & 3

    def upper(g, turn):
        rows = slice(skip, skip + edge)
        return jnp.concatenate(
            [strip(g + groups * ((j + turn) % SLOTS), rows) for j in range(SLOTS)], axis=0
        )

    def lower(g, turn):
        rows = slice(skip + edge, skip + edge + most)
        short = [
            strip(g + groups * ((j + turn) % SLOTS), rows).astype(F32) for j in range(SLOTS)
        ]
        got = mm(jnp.concatenate(short, axis=0).astype(BF16), spread)
        parts = []
        for part in range(3):
            lanes = slice(part * LANES, (part + 1) * LANES)
            rows = []
            for j in range(SLOTS):
                rest = j * most + part * (edge - most)
                rows.append(got[j * most : (j + 1) * most, lanes])
                rows.append(got[rest : rest + edge - most, 3 * LANES :])
            parts.append(jnp.concatenate(rows, axis=0))
        return parts

    def fit(value, turn):
        match = ((row_slot + turn) & 3) == lane_slot[:, : value.shape[1]]
        return jnp.where(match, value, 0.0).astype(BF16)

    for g in range(groups):
        first, second = 1 if g == 0 else 0, -1 if g == last else 0
        plain = upper(g, 0)
        high = mm(upper(g, first) if first else plain, spread)
        low = lower(g, second)
        wf_ref[g, :LANES] = fit(high[:, :wide], first)
        wf_ref[g, LANES:, :LANES] = fit(low[0], second)
        wf_ref[g, LANES:, LANES:] = fit(low[1], second)
        wk_ref[g, :LANES] = fit(high[:, wide:], first)
        wk_ref[g, LANES:, :LANES] = fit(mm_nt(spread_t, plain), second)
        wk_ref[g, LANES:, LANES:] = fit(low[2], second)
        if first or second:
            if first:
                high = mm(plain, spread)
            if second:
                low = lower(g, 0)
            at = 0 if first else 1
            wa_ref[at, :LANES, :LANES] = fit(high[:, :LANES], -second)
            wa_ref[at, :LANES, LANES:] = fit(high[:, LANES:wide], -first)
            wa_ref[at, LANES:, :LANES] = fit(low[0], -second)
            wa_ref[at, LANES:, LANES:] = fit(low[1], -first)

    at = lax.broadcasted_iota(jnp.int32, (1, 2 * wide), 1)
    source = (((at >> 5) & 3) << 7) | ((at >> 7) << 5) | (at & 31)
    order = lax.broadcasted_iota(jnp.int32, (2 * wide, 2 * wide), 0) == source
    order = order.astype(F32).astype(BF16)
    mine = pl.ds(pl.multiple_of(core * chunk, chunk), chunk)
    start = jnp.concatenate(
        [
            jnp.concatenate([strip(g + groups * j, mine) for j in range(SLOTS)], axis=1)
            for g in range(groups)
        ],
        axis=0,
    )
    start = mm(start, order)

    def up(parts, at):
        return [parts[-1]] + parts[:-1] if at == 1 else list(parts)

    def down(parts, at):
        return list(parts) if at == 1 else parts[1:] + [parts[0]]

    def arrive(parts, at, first_up):
        first, second = [v[:, :LANES] for v in parts], [v[:, LANES:] for v in parts]
        if first_up:
            first, second = up(first, at), down(second, at)
        else:
            first, second = down(first, at), up(second, at)
        return [jnp.concatenate([p, q], axis=1).astype(BF16) for p, q in zip(first, second)]

    def turned(parts, first_up):
        def turn(part, half, by):
            halves = [part[:, :LANES], part[:, LANES:]]
            halves[half] = pltpu.roll(halves[half].astype(F32), by, 1).astype(BF16)
            return jnp.concatenate(halves, axis=1)

        parts = list(parts)
        parts[0] = turn(parts[0], 0 if first_up else 1, edge)
        parts[last] = turn(parts[last], 1 if first_up else 0, LANES - edge)
        return parts

    def iterate(base, step, first_up):
        even, odd = [base[g] for g in evens], [base[g] for g in odds]
        ahead, behind = odd, even
        z = arrive(ahead, 1, first_up)
        ahead = [even[i] + step(z[i], g) for i, g in enumerate(evens)]
        for t in range(1, SWEEPS - 2):
            at = (t + 1) % 2
            z = arrive(ahead, at, first_up)
            y = arrive(behind, at, first_up)
            add = odd if at == 0 else even
            both = []
            for i, g in enumerate(odds if at == 0 else evens):
                both.append(step(jnp.concatenate([z[i], y[i]], axis=0), g))
            ahead = [add[i] + v[:chunk] for i, v in enumerate(both)]
            behind = [add[i] + v[chunk:] for i, v in enumerate(both)]
        at = (SWEEPS - 1) % 2
        y = arrive(behind, at, first_up)
        add = odd if at == 0 else even
        behind = [
            add[i] + step(y[i], g) for i, g in enumerate(odds if at == 0 else evens)
        ]
        gets_ahead, gets_behind = arrive(ahead, at, first_up), arrive(behind, 1 - at, first_up)
        got = [None] * groups
        for i, g in enumerate(odds if at == 0 else evens):
            got[g] = gets_ahead[i]
        for i, g in enumerate(evens if at == 0 else odds):
            got[g] = gets_behind[i]
        return got

    base = [start[g * chunk : (g + 1) * chunk, :wide] for g in range(groups)]
    z = iterate(base, lambda v, g: mm(v, wf_ref[g]), True)
    base = [
        start[g * chunk : (g + 1) * chunk, wide:] + mm(z[g], wk_ref[g]) for g in range(groups)
    ]
    ends = {0: wa_ref.at[0], last: wa_ref.at[1]}
    y = iterate(base, lambda v, g: mm_nt(v, ends[g][...] if g in ends else wf_ref[g]), False)
    z, y = turned(z, True), turned(y, False)
    out = jnp.concatenate(
        [jnp.concatenate([z[g], y[g]], axis=1) for g in range(groups)], axis=0
    )
    out = mm(out, order).astype(BF16)
    for g in range(groups):
        for j in range(SLOTS):
            o_ref[g + groups * j] = out[g * chunk : (g + 1) * chunk, j * LANES : (j + 1) * LANES]


def finish(scale_ref, p_ref, b_ref, l_ref, r_ref, zy_ref, o_ref):
    count, block, modes = b_ref.shape
    edge = l_ref.shape[0]
    couple = jnp.concatenate([l_ref[...], r_ref[...]], axis=0).astype(F32).T.astype(BF16)
    couple = jnp.concatenate([couple, jnp.zeros_like(couple)], axis=1)
    pick = (
        lax.broadcasted_iota(jnp.int32, (2 * edge, LANES), 0) + 2 * edge
        == lax.broadcasted_iota(jnp.int32, (2 * edge, LANES), 1)
    ).astype(F32).astype(BF16)
    front = jnp.concatenate([couple, pick], axis=0)
    energies = range(count)
    got = [mm_nt(front, zy_ref[e]) for e in energies]
    rhs = [(b_ref[e].astype(F32) + got[e][:block]).astype(BF16) for e in energies]
    psi = [mm(p_ref[e], rhs[e]).astype(BF16) for e in energies]
    scale = [jnp.concatenate([scale_ref[e]] * (modes // LANES), axis=1) for e in energies]
    source = [psi[e].astype(F32) * scale[e] for e in energies]
    update = [
        jnp.concatenate(
            [
                source[e][:edge] + got[e][block + edge :],
                source[e][edge : block - edge],
                source[e][block - edge :] + got[e][block : block + edge],
            ],
            axis=0,
        ).astype(BF16)
        for e in energies
    ]
    total = jnp.zeros((block, block), F32)
    for e in energies:
        part = mm_nt(update[e], psi[e])
        high = part.astype(BF16)
        low = (part - high.astype(F32)).astype(BF16)
        inverse_t = p_ref[e].T
        total += mm(inverse_t, high) + mm(inverse_t, low)
    total = (total * (-1.0 / modes)).astype(BF16)
    pieces, owned, _ = o_ref.shape
    for k in range(pieces):
        o_ref[k] = total[k * owned : (k + 1) * owned]


SMEM = pl.BlockSpec(memory_space=pltpu.SMEM)
VMEM = pl.BlockSpec(memory_space=pltpu.VMEM)
ANY = pl.BlockSpec(memory_space=pltpu.HBM)
PARAMS = dict(compiler_params=pltpu.CompilerParams(vmem_limit_bytes=24 * 1024 * 1024))


shape = jax.ShapeDtypeStruct


def call_prepare(scalars, inverse, source, left, right, chips, cores, chunk):
    count, block, modes = source.shape
    edge = left.shape[0]
    pieces = (chips, cores * chunk + edge + edge * 3 // 4, 4 * edge)
    return pl.pallas_call(
        prepare,
        out_shape=(shape(pieces, BF16), shape((count, block, LANES), F32)),
        in_specs=[ANY] * 7,
        out_specs=(ANY, ANY),
        scratch_shapes=[
            pltpu.SMEM((count,), F32),
            pltpu.SMEM((1,), jnp.int32),
            pltpu.SMEM((1,), jnp.int32),
            pltpu.VMEM((count, block, block), BF16),
            pltpu.VMEM((count, block, modes), BF16),
            pltpu.VMEM((2 * edge, block), BF16),
            pltpu.VMEM(pieces, BF16),
            pltpu.VMEM((count, block, LANES), F32),
            pltpu.SemaphoreType.DMA((8 + count,)),
        ],
        name="prepare",
    )(*scalars, inverse, source, left, right)


def call_sweeps(core, given, chunk):
    cores, chips, _, lanes = given.shape
    strips = cores * chips
    weights = (strips // SLOTS, 2 * LANES, 2 * LANES)
    return pl.pallas_call(
        sweep_all,
        out_shape=shape((strips, chunk, lanes), BF16),
        in_specs=[SMEM, VMEM],
        out_specs=VMEM,
        scratch_shapes=[
            pltpu.VMEM(weights, BF16),
            pltpu.VMEM((2,) + weights[1:], BF16),
            pltpu.VMEM(weights, BF16),
        ],
        name="sweeps",
        **PARAMS,
    )(core, given)


def call_finish(scale, inverse, source, left, right, columns, energies, owned):
    block = inverse.shape[1]
    return pl.pallas_call(
        finish,
        out_shape=shape((energies, owned, block), BF16),
        in_specs=[VMEM] * 6,
        out_specs=VMEM,
        name="finish",
        **PARAMS,
    )(scale, inverse, source, left, right, columns)


def body(
    inverse_blocks,
    source,
    left_coupling,
    right_coupling,
    energy_weights,
    collector_low,
    collector_high,
):
    count, block, modes = source.shape
    edge = left_coupling.shape[0]
    chips = lax.axis_size("chip")
    cores = lax.axis_size("core")
    strips = chips * cores
    energies = lax.axis_size("energy")
    chunk = count * modes // strips
    owned = block // energies
    scalars = (energy_weights, collector_low, collector_high)

    pieces, scale = call_prepare(
        scalars, inverse_blocks, source, left_coupling, right_coupling, chips, cores, chunk
    )
    mine = lax.all_to_all(pieces, "chip", 0, 0, tiled=True)
    given = lax.all_gather(mine, "core")
    core = lax.axis_index("core").astype(jnp.int32).reshape(1)
    out = call_sweeps(core, given, chunk)
    out = lax.all_to_all(out, ("chip", "core"), 0, 0, tiled=True)
    out = call_finish(
        scale,
        inverse_blocks,
        source,
        left_coupling,
        right_coupling,
        out.reshape(count, modes, 4 * edge),
        energies,
        owned,
    )
    out = lax.all_to_all(out, "energy", 0, 0, tiled=True)
    return jnp.sum(out.astype(F32), axis=0)[None]


def solution(mesh):
    energies, strips = mesh.devices.shape
    cores = 2
    split = jax.sharding.Mesh(
        mesh.devices.reshape(energies, strips // cores, cores), ("energy", "chip", "core")
    )
    width = ("chip", "core")
    placed = (
        P("energy", width, None),
        P("energy", width, None),
        P(width, None),
        P(width, None),
        P("energy"),
        P(width),
        P(width),
    )
    return jax.shard_map(
        body, mesh=split, in_specs=placed, out_specs=P(width, "energy", None), check_vma=False
    )
```

```python
import jax
import jax.numpy as jnp
from jax import lax
from jax.experimental import pallas as pl
from jax.experimental.pallas import tpu as pltpu
from jax.sharding import PartitionSpec as P

SWEEPS = 10
LANES = 128
F32 = jnp.float32
BF16 = jnp.bfloat16


def mm(a, b):
    return jnp.dot(a, b, preferred_element_type=F32)


def mm_nt(a, b):
    return lax.dot_general(a, b, (((1,), (1,)), ((), ())), preferred_element_type=F32)


def pack(step, middle):
    edge = step.shape[0] // 2
    most = edge * 3 // 4
    low = [step[edge:, :edge], step[edge:, edge:], middle[edge:, edge:]]
    rest = jnp.concatenate([v[most:] for v in low], axis=0)
    return jnp.concatenate(
        [
            jnp.concatenate([step[:edge], middle[:edge]], axis=1),
            jnp.concatenate([v[:most] for v in low] + [rest], axis=1),
        ],
        axis=0,
    )


def prepare(
    w_hbm,
    low_hbm,
    high_hbm,
    p_hbm,
    b_hbm,
    l_hbm,
    r_hbm,
    o_hbm,
    scale_hbm,
    w_ref,
    low_ref,
    high_ref,
    p_ref,
    b_ref,
    c_ref,
    o_ref,
    scale_ref,
    sems,
):
    count, block, modes = b_ref.shape
    edge = l_hbm.shape[0]
    fetch = [
        (w_hbm, w_ref),
        (low_hbm, low_ref),
        (high_hbm, high_ref),
        (l_hbm, c_ref.at[pl.ds(0, edge)]),
        (r_hbm, c_ref.at[pl.ds(edge, edge)]),
        (p_hbm, p_ref),
        (b_hbm, b_ref),
    ]
    fetch = [pltpu.make_async_copy(*ends, sems.at[i]) for i, ends in enumerate(fetch)]
    for copy in fetch:
        copy.start()
    for copy in fetch[:3]:
        copy.wait()
    low, high = low_ref[0], high_ref[0]
    at = lax.broadcasted_iota(jnp.int32, (block, LANES), 0)
    inside = (at >= low) & (at < high)
    for e in range(count):
        scale_ref[e] = jnp.where(inside, 2.0 * w_ref[e], 0.0)
    keep = [pltpu.make_async_copy(scale_ref, scale_hbm, sems.at[len(fetch)])]
    keep[0].start()
    at = lax.broadcasted_iota(jnp.int32, (1, block), 1)
    inside = (at >= low) & (at < high)
    for copy in fetch[3:6]:
        copy.wait()
    couple = c_ref[...]
    each = o_ref.shape[0] // count
    chunk = modes // each
    energies = range(count)
    rim = [jnp.concatenate([p_ref[e, block - edge :], p_ref[e, :edge]], axis=0) for e in energies]
    u = [mm_nt(couple, p_ref[e]) for e in energies]
    step = [mm_nt(couple, rim[e]) for e in energies]
    weighted = [jnp.where(inside, u[e] * (2.0 * w_ref[e]), 0.0).astype(BF16) for e in energies]
    outer = [mm(weighted[e], p_ref[e]).astype(BF16) for e in energies]
    middle = [mm_nt(weighted[e], u[e].astype(BF16)) for e in energies]
    fetch[6].wait()
    for e in energies:
        rows = mm(jnp.concatenate([rim[e], outer[e]], axis=0), b_ref[e])
        columns = rows.T.astype(BF16)
        exact = pack(step[e], middle[e])
        left = jnp.zeros_like(exact)
        for k in range(each):
            left += exact
            rounded = left.astype(BF16)
            left -= rounded.astype(F32)
            o_ref[e * each + k, chunk:] = rounded
            o_ref[e * each + k, :chunk] = columns[k * chunk : (k + 1) * chunk]
        part = pl.ds(e * each, each)
        keep.append(
            pltpu.make_async_copy(o_ref.at[part], o_hbm.at[part], sems.at[len(fetch) + 1 + e])
        )
        keep[-1].start()
    for copy in keep:
        copy.wait()


SLOTS = 4


def sweep_all(core_ref, x_ref, o_ref, wf_ref, wa_ref, wk_ref):
    chips, chunk, _ = o_ref.shape
    strips = chips * x_ref.shape[0]
    edge = LANES // SLOTS
    most = edge * 3 // 4
    groups = strips // SLOTS
    wide = 2 * LANES
    last = groups - 1
    core = core_ref[0]
    skip = chunk
    evens, odds = range(0, groups, 2), range(1, groups, 2)

    def strip(s, rows):
        return x_ref[s % 2, s // 2, rows]

    at = lax.broadcasted_iota(jnp.int32, (1, 2 * wide), 1)
    source = ((at >> 7) << 5) | (at & 31)
    spread = lax.broadcasted_iota(jnp.int32, (LANES, 2 * wide), 0) == source
    spread = spread.astype(F32).astype(BF16)
    source = (lax.broadcasted_iota(jnp.int32, (LANES, 1), 0) & 31) | 96
    spread_t = lax.broadcasted_iota(jnp.int32, (LANES, LANES), 1) == source
    spread_t = spread_t.astype(F32).astype(BF16)
    row_slot = lax.broadcasted_iota(jnp.int32, (LANES, 1), 0) >> 5
    lane_slot = (lax.broadcasted_iota(jnp.int32, (1, wide), 1) >> 5) & 3

    def upper(g, turn):
        rows = slice(skip, skip + edge)
        return jnp.concatenate(
            [strip(g + groups * ((j + turn) % SLOTS), rows) for j in range(SLOTS)], axis=0
        )

    def lower(g, turn):
        rows = slice(skip + edge, skip + edge + most)
        short = [
            strip(g + groups * ((j + turn) % SLOTS), rows).astype(F32) for j in range(SLOTS)
        ]
        got = mm(jnp.concatenate(short, axis=0).astype(BF16), spread)
        parts = []
        for part in range(3):
            lanes = slice(part * LANES, (part + 1) * LANES)
            rows = []
            for j in range(SLOTS):
                rest = j * most + part * (edge - most)
                rows.append(got[j * most : (j + 1) * most, lanes])
                rows.append(got[rest : rest + edge - most, 3 * LANES :])
            parts.append(jnp.concatenate(rows, axis=0))
        return parts

    def fit(value, turn):
        match = ((row_slot + turn) & 3) == lane_slot[:, : value.shape[1]]
        return jnp.where(match, value, 0.0).astype(BF16)

    for g in range(groups):
        first, second = 1 if g == 0 else 0, -1 if g == last else 0
        plain = upper(g, 0)
        high = mm(upper(g, first) if first else plain, spread)
        low = lower(g, second)
        wf_ref[g, :LANES] = fit(high[:, :wide], first)
        wf_ref[g, LANES:, :LANES] = fit(low[0], second)
        wf_ref[g, LANES:, LANES:] = fit(low[1], second)
        wk_ref[g, :LANES] = fit(high[:, wide:], first)
        wk_ref[g, LANES:, :LANES] = fit(mm_nt(spread_t, plain), second)
        wk_ref[g, LANES:, LANES:] = fit(low[2], second)
        if first or second:
            if first:
                high = mm(plain, spread)
            if second:
                low = lower(g, 0)
            at = 0 if first else 1
            wa_ref[at, :LANES, :LANES] = fit(high[:, :LANES], -second)
            wa_ref[at, :LANES, LANES:] = fit(high[:, LANES:wide], -first)
            wa_ref[at, LANES:, :LANES] = fit(low[0], -second)
            wa_ref[at, LANES:, LANES:] = fit(low[1], -first)

    at = lax.broadcasted_iota(jnp.int32, (1, 2 * wide), 1)
    source = (((at >> 5) & 3) << 7) | ((at >> 7) << 5) | (at & 31)
    order = lax.broadcasted_iota(jnp.int32, (2 * wide, 2 * wide), 0) == source
    order = order.astype(F32).astype(BF16)
    start = jnp.concatenate(
        [
            jnp.concatenate([strip(g + groups * j, slice(chunk)) for j in range(SLOTS)], axis=1)
            for g in range(groups)
        ],
        axis=0,
    )
    start = mm(start, order)

    def up(parts, at):
        return [parts[-1]] + parts[:-1] if at == 1 else list(parts)

    def down(parts, at):
        return list(parts) if at == 1 else parts[1:] + [parts[0]]

    def arrive(parts, at, first_up):
        first, second = [v[:, :LANES] for v in parts], [v[:, LANES:] for v in parts]
        if first_up:
            first, second = up(first, at), down(second, at)
        else:
            first, second = down(first, at), up(second, at)
        return [jnp.concatenate([p, q], axis=1).astype(BF16) for p, q in zip(first, second)]

    def turned(parts, first_up):
        def turn(part, half, by):
            halves = [part[:, :LANES], part[:, LANES:]]
            halves[half] = pltpu.roll(halves[half].astype(F32), by, 1).astype(BF16)
            return jnp.concatenate(halves, axis=1)

        parts = list(parts)
        parts[0] = turn(parts[0], 0 if first_up else 1, edge)
        parts[last] = turn(parts[last], 1 if first_up else 0, LANES - edge)
        return parts

    def iterate(base, step, first_up):
        even, odd = [base[g] for g in evens], [base[g] for g in odds]
        ahead, behind = odd, even
        z = arrive(ahead, 1, first_up)
        ahead = [even[i] + step(z[i], g) for i, g in enumerate(evens)]
        for t in range(1, SWEEPS - 2):
            at = (t + 1) % 2
            z = arrive(ahead, at, first_up)
            y = arrive(behind, at, first_up)
            add = odd if at == 0 else even
            both = []
            for i, g in enumerate(odds if at == 0 else evens):
                both.append(step(jnp.concatenate([z[i], y[i]], axis=0), g))
            ahead = [add[i] + v[:chunk] for i, v in enumerate(both)]
            behind = [add[i] + v[chunk:] for i, v in enumerate(both)]
        at = (SWEEPS - 1) % 2
        y = arrive(behind, at, first_up)
        add = odd if at == 0 else even
        behind = [
            add[i] + step(y[i], g) for i, g in enumerate(odds if at == 0 else evens)
        ]
        gets_ahead, gets_behind = arrive(ahead, at, first_up), arrive(behind, 1 - at, first_up)
        got = [None] * groups
        for i, g in enumerate(odds if at == 0 else evens):
            got[g] = gets_ahead[i]
        for i, g in enumerate(evens if at == 0 else odds):
            got[g] = gets_behind[i]
        return got

    base = [start[g * chunk : (g + 1) * chunk, :wide] for g in range(groups)]
    z = iterate(base, lambda v, g: mm(v, wf_ref[g]), True)
    base = [
        start[g * chunk : (g + 1) * chunk, wide:] + mm(z[g], wk_ref[g]) for g in range(groups)
    ]
    ends = {0: wa_ref.at[0], last: wa_ref.at[1]}
    y = iterate(base, lambda v, g: mm_nt(v, ends[g][...] if g in ends else wf_ref[g]), False)
    out = [jnp.concatenate(v, axis=1) for v in zip(turned(z, True), turned(y, False))]
    out = [jnp.where(core == 0, out[g], out[g + 1]) for g in evens]
    out = mm(jnp.concatenate(out, axis=0), order).astype(BF16)
    for i, g in enumerate(evens):
        for j in range(SLOTS):
            o_ref[(g + groups * j) // 2] = out[
                i * chunk : (i + 1) * chunk, j * LANES : (j + 1) * LANES
            ]


def finish(scale_ref, p_ref, b_ref, l_ref, r_ref, zy_ref, o_ref):
    count, block, modes = b_ref.shape
    edge = l_ref.shape[0]
    couple = jnp.concatenate([l_ref[...], r_ref[...]], axis=0).astype(F32).T.astype(BF16)
    couple = jnp.concatenate([couple, jnp.zeros_like(couple)], axis=1)
    pick = (
        lax.broadcasted_iota(jnp.int32, (2 * edge, LANES), 0) + 2 * edge
        == lax.broadcasted_iota(jnp.int32, (2 * edge, LANES), 1)
    ).astype(F32).astype(BF16)
    front = jnp.concatenate([couple, pick], axis=0)
    energies = range(count)
    got = [mm_nt(front, zy_ref[e]) for e in energies]
    rhs = [(b_ref[e].astype(F32) + got[e][:block]).astype(BF16) for e in energies]
    psi = [mm(p_ref[e], rhs[e]).astype(BF16) for e in energies]
    scale = [jnp.concatenate([scale_ref[e]] * (modes // LANES), axis=1) for e in energies]
    source = [psi[e].astype(F32) * scale[e] for e in energies]
    update = [
        jnp.concatenate(
            [
                source[e][:edge] + got[e][block + edge :],
                source[e][edge : block - edge],
                source[e][block - edge :] + got[e][block : block + edge],
            ],
            axis=0,
        ).astype(BF16)
        for e in energies
    ]
    total = jnp.zeros((block, block), F32)
    for e in energies:
        part = mm_nt(update[e], psi[e])
        high = part.astype(BF16)
        low = (part - high.astype(F32)).astype(BF16)
        inverse_t = p_ref[e].T
        total += mm(inverse_t, high) + mm(inverse_t, low)
    total = (total * (-1.0 / modes)).astype(BF16)
    pieces, owned, _ = o_ref.shape
    for k in range(pieces):
        o_ref[k] = total[k * owned : (k + 1) * owned]


SMEM = pl.BlockSpec(memory_space=pltpu.SMEM)
VMEM = pl.BlockSpec(memory_space=pltpu.VMEM)
ANY = pl.BlockSpec(memory_space=pltpu.HBM)
PARAMS = dict(compiler_params=pltpu.CompilerParams(vmem_limit_bytes=24 * 1024 * 1024))


shape = jax.ShapeDtypeStruct


def call_prepare(scalars, inverse, source, left, right, chips):
    count, block, modes = source.shape
    edge = left.shape[0]
    pieces = (chips, count * modes // chips + edge + edge * 3 // 4, 4 * edge)
    return pl.pallas_call(
        prepare,
        out_shape=(shape(pieces, BF16), shape((count, block, LANES), F32)),
        in_specs=[ANY] * 7,
        out_specs=(ANY, ANY),
        scratch_shapes=[
            pltpu.SMEM((count,), F32),
            pltpu.SMEM((1,), jnp.int32),
            pltpu.SMEM((1,), jnp.int32),
            pltpu.VMEM((count, block, block), BF16),
            pltpu.VMEM((count, block, modes), BF16),
            pltpu.VMEM((2 * edge, block), BF16),
            pltpu.VMEM(pieces, BF16),
            pltpu.VMEM((count, block, LANES), F32),
            pltpu.SemaphoreType.DMA((8 + count,)),
        ],
        name="prepare",
    )(*scalars, inverse, source, left, right)


def call_sweeps(core, given, chunk):
    cores, chips, _, lanes = given.shape
    weights = (cores * chips // SLOTS, 2 * LANES, 2 * LANES)
    return pl.pallas_call(
        sweep_all,
        out_shape=shape((chips, chunk, lanes), BF16),
        in_specs=[SMEM, VMEM],
        out_specs=VMEM,
        scratch_shapes=[
            pltpu.VMEM(weights, BF16),
            pltpu.VMEM((2,) + weights[1:], BF16),
            pltpu.VMEM(weights, BF16),
        ],
        name="sweeps",
        **PARAMS,
    )(core, given)


def call_finish(scale, inverse, source, left, right, columns, energies, owned):
    block = inverse.shape[1]
    return pl.pallas_call(
        finish,
        out_shape=shape((energies, owned, block), BF16),
        in_specs=[VMEM] * 6,
        out_specs=VMEM,
        name="finish",
        **PARAMS,
    )(scale, inverse, source, left, right, columns)


def body(
    inverse_blocks,
    source,
    left_coupling,
    right_coupling,
    energy_weights,
    collector_low,
    collector_high,
):
    count, block, modes = source.shape
    edge = left_coupling.shape[0]
    chips = lax.axis_size("chip")
    energies = lax.axis_size("energy")
    chunk = count * modes // chips
    owned = block // energies
    scalars = (energy_weights, collector_low, collector_high)

    pieces, scale = call_prepare(
        scalars, inverse_blocks, source, left_coupling, right_coupling, chips
    )
    mine = lax.all_to_all(pieces, "chip", 0, 0, tiled=True)
    given = lax.all_gather(mine, "core")
    core = lax.axis_index("core").astype(jnp.int32).reshape(1)
    out = call_sweeps(core, given, chunk)
    out = lax.all_to_all(out, "chip", 0, 0, tiled=True)
    out = call_finish(
        scale,
        inverse_blocks,
        source,
        left_coupling,
        right_coupling,
        out.reshape(count, modes, 4 * edge),
        energies,
        owned,
    )
    out = lax.all_to_all(out, "energy", 0, 0, tiled=True)
    return jnp.sum(out.astype(F32), axis=0)[None]


def solution(mesh):
    energies, strips = mesh.devices.shape
    cores = 2
    split = jax.sharding.Mesh(
        mesh.devices.reshape(energies, strips // cores, cores), ("energy", "chip", "core")
    )
    width = ("chip", "core")
    placed = (
        P("energy", width, None),
        P("energy", width, None),
        P(width, None),
        P(width, None),
        P("energy"),
        P(width),
        P(width),
    )
    return jax.shard_map(
        body, mesh=split, in_specs=placed, out_specs=P(width, "energy", None), check_vma=False
    )
```

```python
import jax
import jax.numpy as jnp
from jax import lax
from jax.experimental import pallas as pl
from jax.experimental.pallas import tpu as pltpu
from jax.sharding import PartitionSpec as P

SWEEPS = 10
LANES = 128
F32 = jnp.float32
BF16 = jnp.bfloat16


def mm(a, b):
    return jnp.dot(a, b, preferred_element_type=F32)


def mm_nt(a, b):
    return lax.dot_general(a, b, (((1,), (1,)), ((), ())), preferred_element_type=F32)


def pack(step, middle):
    edge = step.shape[0] // 2
    most = edge * 3 // 4
    low = [step[edge:, :edge], step[edge:, edge:], middle[edge:, edge:]]
    rest = jnp.concatenate([v[most:] for v in low], axis=0)
    return jnp.concatenate(
        [
            jnp.concatenate([step[:edge], middle[:edge]], axis=1),
            jnp.concatenate([v[:most] for v in low] + [rest], axis=1),
        ],
        axis=0,
    )


def prepare(
    w_hbm,
    low_ref,
    high_ref,
    p_hbm,
    b_hbm,
    l_hbm,
    r_hbm,
    o_ref,
    scale_ref,
    w_ref,
    p_ref,
    b_ref,
    c_ref,
    sems,
):
    count, block, modes = b_ref.shape
    edge = l_hbm.shape[0]
    fetch = [
        (w_hbm, w_ref),
        (l_hbm, c_ref.at[pl.ds(0, edge)]),
        (r_hbm, c_ref.at[pl.ds(edge, edge)]),
        (p_hbm, p_ref),
        (b_hbm, b_ref),
    ]
    fetch = [pltpu.make_async_copy(*ends, sems.at[i]) for i, ends in enumerate(fetch)]
    for copy in fetch:
        copy.start()
    fetch[0].wait()
    low, high = low_ref[0], high_ref[0]
    at = lax.broadcasted_iota(jnp.int32, (block, LANES), 0)
    inside = (at >= low) & (at < high)
    for e in range(count):
        scale_ref[e] = jnp.where(inside, 2.0 * w_ref[e], 0.0)
    at = lax.broadcasted_iota(jnp.int32, (1, block), 1)
    inside = (at >= low) & (at < high)
    for copy in fetch[1:4]:
        copy.wait()
    couple = c_ref[...]
    each = o_ref.shape[0] // count
    chunk = modes // each
    energies = range(count)
    rim = [jnp.concatenate([p_ref[e, block - edge :], p_ref[e, :edge]], axis=0) for e in energies]
    u = [mm_nt(couple, p_ref[e]) for e in energies]
    step = [mm_nt(couple, rim[e]) for e in energies]
    weighted = [jnp.where(inside, u[e] * (2.0 * w_ref[e]), 0.0).astype(BF16) for e in energies]
    outer = [mm(weighted[e], p_ref[e]).astype(BF16) for e in energies]
    middle = [mm_nt(weighted[e], u[e].astype(BF16)) for e in energies]
    fetch[4].wait()
    for e in energies:
        rows = mm(jnp.concatenate([rim[e], outer[e]], axis=0), b_ref[e])
        columns = rows.T.astype(BF16)
        exact = pack(step[e], middle[e])
        left = jnp.zeros_like(exact)
        for k in range(each):
            left += exact
            rounded = left.astype(BF16)
            left -= rounded.astype(F32)
            o_ref[e * each + k, chunk:] = rounded
            o_ref[e * each + k, :chunk] = columns[k * chunk : (k + 1) * chunk]


SLOTS = 4


def sweep_all(x_ref, o_ref, wf_ref, wa_ref, wk_ref):
    chips, chunk, _ = o_ref.shape
    strips = chips * x_ref.shape[0]
    edge = LANES // SLOTS
    most = edge * 3 // 4
    groups = strips // SLOTS
    wide = 2 * LANES
    last = groups - 1
    core = lax.axis_index("core")
    skip = chunk
    evens, odds = range(0, groups, 2), range(1, groups, 2)

    def strip(s, rows):
        return x_ref[s % 2, s // 2, rows]

    at = lax.broadcasted_iota(jnp.int32, (1, 2 * wide), 1)
    source = ((at >> 7) << 5) | (at & 31)
    spread = lax.broadcasted_iota(jnp.int32, (LANES, 2 * wide), 0) == source
    spread = spread.astype(F32).astype(BF16)
    source = (lax.broadcasted_iota(jnp.int32, (LANES, 1), 0) & 31) | 96
    spread_t = lax.broadcasted_iota(jnp.int32, (LANES, LANES), 1) == source
    spread_t = spread_t.astype(F32).astype(BF16)
    row_slot = lax.broadcasted_iota(jnp.int32, (LANES, 1), 0) >> 5
    lane_slot = (lax.broadcasted_iota(jnp.int32, (1, wide), 1) >> 5) & 3

    def upper(g, turn):
        rows = slice(skip, skip + edge)
        return jnp.concatenate(
            [strip(g + groups * ((j + turn) % SLOTS), rows) for j in range(SLOTS)], axis=0
        )

    def lower(g, turn):
        rows = slice(skip + edge, skip + edge + most)
        short = [
            strip(g + groups * ((j + turn) % SLOTS), rows).astype(F32) for j in range(SLOTS)
        ]
        got = mm(jnp.concatenate(short, axis=0).astype(BF16), spread)
        parts = []
        for part in range(3):
            lanes = slice(part * LANES, (part + 1) * LANES)
            rows = []
            for j in range(SLOTS):
                rest = j * most + part * (edge - most)
                rows.append(got[j * most : (j + 1) * most, lanes])
                rows.append(got[rest : rest + edge - most, 3 * LANES :])
            parts.append(jnp.concatenate(rows, axis=0))
        return parts

    def fit(value, turn):
        match = ((row_slot + turn) & 3) == lane_slot[:, : value.shape[1]]
        return jnp.where(match, value, 0.0).astype(BF16)

    for g in range(groups):
        first, second = 1 if g == 0 else 0, -1 if g == last else 0
        plain = upper(g, 0)
        high = mm(upper(g, first) if first else plain, spread)
        low = lower(g, second)
        wf_ref[g, :LANES] = fit(high[:, :wide], first)
        wf_ref[g, LANES:, :LANES] = fit(low[0], second)
        wf_ref[g, LANES:, LANES:] = fit(low[1], second)
        wk_ref[g, :LANES] = fit(high[:, wide:], first)
        wk_ref[g, LANES:, :LANES] = fit(mm_nt(spread_t, plain), second)
        wk_ref[g, LANES:, LANES:] = fit(low[2], second)
        if first or second:
            if first:
                high = mm(plain, spread)
            if second:
                low = lower(g, 0)
            at = 0 if first else 1
            wa_ref[at, :LANES, :LANES] = fit(high[:, :LANES], -second)
            wa_ref[at, :LANES, LANES:] = fit(high[:, LANES:wide], -first)
            wa_ref[at, LANES:, :LANES] = fit(low[0], -second)
            wa_ref[at, LANES:, LANES:] = fit(low[1], -first)

    at = lax.broadcasted_iota(jnp.int32, (1, 2 * wide), 1)
    source = (((at >> 5) & 3) << 7) | ((at >> 7) << 5) | (at & 31)
    order = lax.broadcasted_iota(jnp.int32, (2 * wide, 2 * wide), 0) == source
    order = order.astype(F32).astype(BF16)
    start = jnp.concatenate(
        [
            jnp.concatenate([strip(g + groups * j, slice(chunk)) for j in range(SLOTS)], axis=1)
            for g in range(groups)
        ],
        axis=0,
    )
    start = mm(start, order)

    def up(parts, at):
        return [parts[-1]] + parts[:-1] if at == 1 else list(parts)

    def down(parts, at):
        return list(parts) if at == 1 else parts[1:] + [parts[0]]

    def arrive(parts, at, first_up):
        first, second = [v[:, :LANES] for v in parts], [v[:, LANES:] for v in parts]
        if first_up:
            first, second = up(first, at), down(second, at)
        else:
            first, second = down(first, at), up(second, at)
        return [jnp.concatenate([p, q], axis=1).astype(BF16) for p, q in zip(first, second)]

    def turned(parts, first_up):
        def turn(part, half, by):
            halves = [part[:, :LANES], part[:, LANES:]]
            halves[half] = pltpu.roll(halves[half].astype(F32), by, 1).astype(BF16)
            return jnp.concatenate(halves, axis=1)

        parts = list(parts)
        parts[0] = turn(parts[0], 0 if first_up else 1, edge)
        parts[last] = turn(parts[last], 1 if first_up else 0, LANES - edge)
        return parts

    def iterate(base, step, first_up):
        even, odd = [base[g] for g in evens], [base[g] for g in odds]
        ahead, behind = odd, even
        z = arrive(ahead, 1, first_up)
        ahead = [even[i] + step(z[i], g) for i, g in enumerate(evens)]
        for t in range(1, SWEEPS - 2):
            at = (t + 1) % 2
            z = arrive(ahead, at, first_up)
            y = arrive(behind, at, first_up)
            add = odd if at == 0 else even
            both = []
            for i, g in enumerate(odds if at == 0 else evens):
                both.append(step(jnp.concatenate([z[i], y[i]], axis=0), g))
            ahead = [add[i] + v[:chunk] for i, v in enumerate(both)]
            behind = [add[i] + v[chunk:] for i, v in enumerate(both)]
        at = (SWEEPS - 1) % 2
        y = arrive(behind, at, first_up)
        add = odd if at == 0 else even
        behind = [
            add[i] + step(y[i], g) for i, g in enumerate(odds if at == 0 else evens)
        ]
        gets_ahead, gets_behind = arrive(ahead, at, first_up), arrive(behind, 1 - at, first_up)
        got = [None] * groups
        for i, g in enumerate(odds if at == 0 else evens):
            got[g] = gets_ahead[i]
        for i, g in enumerate(evens if at == 0 else odds):
            got[g] = gets_behind[i]
        return got

    base = [start[g * chunk : (g + 1) * chunk, :wide] for g in range(groups)]
    z = iterate(base, lambda v, g: mm(v, wf_ref[g]), True)
    base = [
        start[g * chunk : (g + 1) * chunk, wide:] + mm(z[g], wk_ref[g]) for g in range(groups)
    ]
    ends = {0: wa_ref.at[0], last: wa_ref.at[1]}
    y = iterate(base, lambda v, g: mm_nt(v, ends[g][...] if g in ends else wf_ref[g]), False)
    out = [jnp.concatenate(v, axis=1) for v in zip(turned(z, True), turned(y, False))]
    out = [jnp.where(core == 0, out[g], out[g + 1]) for g in evens]
    out = mm(jnp.concatenate(out, axis=0), order).astype(BF16)
    for i, g in enumerate(evens):
        for j in range(SLOTS):
            o_ref[(g + groups * j) // 2] = out[
                i * chunk : (i + 1) * chunk, j * LANES : (j + 1) * LANES
            ]


def finish(scale_ref, p_ref, b_ref, l_ref, r_ref, zy_ref, o_ref):
    count, block, modes = b_ref.shape
    edge = l_ref.shape[0]
    couple = jnp.concatenate([l_ref[...], r_ref[...]], axis=0).astype(F32).T.astype(BF16)
    couple = jnp.concatenate([couple, jnp.zeros_like(couple)], axis=1)
    pick = (
        lax.broadcasted_iota(jnp.int32, (2 * edge, LANES), 0) + 2 * edge
        == lax.broadcasted_iota(jnp.int32, (2 * edge, LANES), 1)
    ).astype(F32).astype(BF16)
    front = jnp.concatenate([couple, pick], axis=0)
    energies = range(count)
    got = [mm_nt(front, zy_ref[e]) for e in energies]
    rhs = [(b_ref[e].astype(F32) + got[e][:block]).astype(BF16) for e in energies]
    psi = [mm(p_ref[e], rhs[e]).astype(BF16) for e in energies]
    scale = [jnp.concatenate([scale_ref[e]] * (modes // LANES), axis=1) for e in energies]
    source = [psi[e].astype(F32) * scale[e] for e in energies]
    update = [
        jnp.concatenate(
            [
                source[e][:edge] + got[e][block + edge :],
                source[e][edge : block - edge],
                source[e][block - edge :] + got[e][block : block + edge],
            ],
            axis=0,
        ).astype(BF16)
        for e in energies
    ]
    total = jnp.zeros((block, block), F32)
    for e in energies:
        part = mm_nt(update[e], psi[e])
        high = part.astype(BF16)
        low = (part - high.astype(F32)).astype(BF16)
        inverse_t = p_ref[e].T
        total += mm(inverse_t, high) + mm(inverse_t, low)
    total = (total * (-1.0 / modes)).astype(BF16)
    pieces, owned, _ = o_ref.shape
    for k in range(pieces):
        o_ref[k] = total[k * owned : (k + 1) * owned]


SMEM = pl.BlockSpec(memory_space=pltpu.SMEM)
VMEM = pl.BlockSpec(memory_space=pltpu.VMEM)
ANY = pl.BlockSpec(memory_space=pltpu.HBM)
PARAMS = dict(compiler_params=pltpu.CompilerParams(vmem_limit_bytes=24 * 1024 * 1024))


shape = jax.ShapeDtypeStruct


def call_prepare(scalars, inverse, source, left, right, chips):
    count, block, modes = source.shape
    edge = left.shape[0]
    held = [pltpu.with_memory_space_constraint(scalars[0], pltpu.HBM)]
    tensors = [
        pltpu.with_memory_space_constraint(v, pltpu.HBM) for v in (inverse, source, left, right)
    ]
    pieces = (chips, count * modes // chips + edge + edge * 3 // 4, 4 * edge)
    return pl.pallas_call(
        prepare,
        out_shape=(pltpu.VMEM(pieces, BF16), pltpu.VMEM((count, block, LANES), F32)),
        in_specs=[ANY, SMEM, SMEM] + [ANY] * 4,
        out_specs=(VMEM, VMEM),
        scratch_shapes=[
            pltpu.SMEM((count,), F32),
            pltpu.VMEM((count, block, block), BF16),
            pltpu.VMEM((count, block, modes), BF16),
            pltpu.VMEM((2 * edge, block), BF16),
            pltpu.SemaphoreType.DMA((5,)),
        ],
        name="prepare",
        **PARAMS,
    )(*held, *scalars[1:], *tensors)


def call_sweeps(given, chunk):
    cores, chips, _, lanes = given.shape
    weights = (cores * chips // SLOTS, 2 * LANES, 2 * LANES)
    return pl.pallas_call(
        sweep_all,
        out_shape=shape((chips, chunk, lanes), BF16),
        in_specs=[VMEM],
        out_specs=VMEM,
        scratch_shapes=[
            pltpu.VMEM(weights, BF16),
            pltpu.VMEM((2,) + weights[1:], BF16),
            pltpu.VMEM(weights, BF16),
        ],
        name="sweeps",
        **PARAMS,
    )(given)


def call_finish(scale, inverse, source, left, right, columns, energies, owned):
    block = inverse.shape[1]
    return pl.pallas_call(
        finish,
        out_shape=shape((energies, owned, block), BF16),
        in_specs=[VMEM] * 6,
        out_specs=VMEM,
        name="finish",
        **PARAMS,
    )(scale, inverse, source, left, right, columns)


def body(
    inverse_blocks,
    source,
    left_coupling,
    right_coupling,
    energy_weights,
    collector_low,
    collector_high,
):
    count, block, modes = source.shape
    edge = left_coupling.shape[0]
    chips = lax.axis_size("chip")
    energies = lax.axis_size("energy")
    chunk = count * modes // chips
    owned = block // energies
    scalars = (energy_weights, collector_low, collector_high)

    pieces, scale = call_prepare(
        scalars, inverse_blocks, source, left_coupling, right_coupling, chips
    )
    mine = lax.all_to_all(pieces, "chip", 0, 0, tiled=True)
    given = lax.all_gather(mine, "core")
    out = call_sweeps(given, chunk)
    out = lax.all_to_all(out, "chip", 0, 0, tiled=True)
    out = call_finish(
        scale,
        inverse_blocks,
        source,
        left_coupling,
        right_coupling,
        out.reshape(count, modes, 4 * edge),
        energies,
        owned,
    )
    out = lax.all_to_all(out, "energy", 0, 0, tiled=True)
    return jnp.sum(out.astype(F32), axis=0)[None]


def solution(mesh):
    energies, strips = mesh.devices.shape
    cores = 2
    split = jax.sharding.Mesh(
        mesh.devices.reshape(energies, strips // cores, cores), ("energy", "chip", "core")
    )
    width = ("chip", "core")
    placed = (
        P("energy", width, None),
        P("energy", width, None),
        P(width, None),
        P(width, None),
        P("energy"),
        P(width),
        P(width),
    )
    return jax.shard_map(
        body, mesh=split, in_specs=placed, out_specs=P(width, "energy", None), check_vma=False
    )
```

```python
import functools

import jax
import jax.numpy as jnp
from jax import lax
from jax.experimental import pallas as pl
from jax.experimental.pallas import tpu as pltpu
from jax.sharding import PartitionSpec as P

SWEEPS = 10
LANES = 128
F32 = jnp.float32
BF16 = jnp.bfloat16


def mm(a, b):
    return jnp.dot(a, b, preferred_element_type=F32)


def mm_nt(a, b):
    return lax.dot_general(a, b, (((1,), (1,)), ((), ())), preferred_element_type=F32)


SLOTS = 4


def own_slot(chips):
    return lax.axis_index("chip") // (chips // SLOTS)


def pack(step, middle):
    edge = step.shape[0] // 2
    most = edge * 3 // 4
    low = [step[edge:, :edge], step[edge:, edge:], middle[edge:, edge:]]
    rest = jnp.concatenate([v[most:] for v in low], axis=0)
    return jnp.concatenate(
        [
            jnp.concatenate([step[:edge], middle[:edge]], axis=1),
            jnp.concatenate([v[:most] for v in low] + [rest], axis=1),
        ],
        axis=0,
    )


def prepare(
    w_hbm,
    low_ref,
    high_ref,
    p_hbm,
    b_hbm,
    l_hbm,
    r_hbm,
    o_ref,
    scale_ref,
    w_ref,
    p_ref,
    b_ref,
    c_ref,
    q_ref,
    sems,
):
    count, block, modes = b_ref.shape
    edge = l_hbm.shape[0]
    fetch = [
        (w_hbm, w_ref),
        (l_hbm, c_ref.at[pl.ds(0, edge)]),
        (r_hbm, c_ref.at[pl.ds(edge, edge)]),
        (p_hbm, p_ref),
        (b_hbm, b_ref),
    ]
    fetch = [pltpu.make_async_copy(*ends, sems.at[i]) for i, ends in enumerate(fetch)]
    for copy in fetch:
        copy.start()
    fetch[0].wait()
    low, high = low_ref[0], high_ref[0]
    at = lax.broadcasted_iota(jnp.int32, (block, LANES), 0)
    inside = (at >= low) & (at < high)
    for e in range(count):
        scale_ref[e] = jnp.where(inside, 2.0 * w_ref[e], 0.0)
    at = lax.broadcasted_iota(jnp.int32, (1, block), 1)
    inside = (at >= low) & (at < high)
    for copy in fetch[1:4]:
        copy.wait()
    couple = c_ref[...]
    each = o_ref.shape[0] // count
    chunk = modes // each
    energies = range(count)
    rim = [jnp.concatenate([p_ref[e, block - edge :], p_ref[e, :edge]], axis=0) for e in energies]
    u = [mm_nt(couple, p_ref[e]) for e in energies]
    step = [mm_nt(couple, rim[e]) for e in energies]
    weighted = [jnp.where(inside, u[e] * (2.0 * w_ref[e]), 0.0).astype(BF16) for e in energies]
    outer = [mm(weighted[e], p_ref[e]).astype(BF16) for e in energies]
    middle = [mm_nt(weighted[e], u[e].astype(BF16)) for e in energies]
    slot = own_slot(o_ref.shape[0])
    for e in energies:
        blocks = [rim[e][:edge], rim[e][edge:], outer[e][:edge], outer[e][edge:]]
        for i, rows in enumerate(blocks):
            at = pl.multiple_of(((slot + i) & 3) * edge, edge)
            q_ref[e, pl.ds(at, edge)] = rows
    fetch[4].wait()
    for e in energies:
        rows = mm(q_ref[e], b_ref[e])
        columns = rows.T.astype(BF16)
        exact = pack(step[e], middle[e])
        left = jnp.zeros_like(exact)
        for k in range(each):
            left += exact
            rounded = left.astype(BF16)
            left -= rounded.astype(F32)
            o_ref[e * each + k, chunk:] = rounded
            o_ref[e * each + k, :chunk] = columns[k * chunk : (k + 1) * chunk]


def sweep_all(x_ref, o_ref, wf_ref, wa_ref, wk_ref):
    chips, chunk, _ = o_ref.shape
    strips = chips * x_ref.shape[0]
    edge = LANES // SLOTS
    most = edge * 3 // 4
    groups = strips // SLOTS
    wide = 2 * LANES
    last = groups - 1
    core = lax.axis_index("core")
    skip = chunk
    evens, odds = range(0, groups, 2), range(1, groups, 2)

    def strip(s, rows):
        return x_ref[s % 2, s // 2, rows]

    at = lax.broadcasted_iota(jnp.int32, (1, 2 * wide), 1)
    source = ((at >> 7) << 5) | (at & 31)
    spread = lax.broadcasted_iota(jnp.int32, (LANES, 2 * wide), 0) == source
    spread = spread.astype(F32).astype(BF16)
    source = (lax.broadcasted_iota(jnp.int32, (LANES, 1), 0) & 31) | 96
    spread_t = lax.broadcasted_iota(jnp.int32, (LANES, LANES), 1) == source
    spread_t = spread_t.astype(F32).astype(BF16)
    row_slot = lax.broadcasted_iota(jnp.int32, (LANES, 1), 0) >> 5
    lane_slot = (lax.broadcasted_iota(jnp.int32, (1, wide), 1) >> 5) & 3

    def upper(g, turn):
        rows = slice(skip, skip + edge)
        return jnp.concatenate(
            [strip(g + groups * ((j + turn) % SLOTS), rows) for j in range(SLOTS)], axis=0
        )

    def lower(g, turn):
        rows = slice(skip + edge, skip + edge + most)
        short = [
            strip(g + groups * ((j + turn) % SLOTS), rows).astype(F32) for j in range(SLOTS)
        ]
        got = mm(jnp.concatenate(short, axis=0).astype(BF16), spread)
        parts = []
        for part in range(3):
            lanes = slice(part * LANES, (part + 1) * LANES)
            rows = []
            for j in range(SLOTS):
                rest = j * most + part * (edge - most)
                rows.append(got[j * most : (j + 1) * most, lanes])
                rows.append(got[rest : rest + edge - most, 3 * LANES :])
            parts.append(jnp.concatenate(rows, axis=0))
        return parts

    def fit(value, turn):
        match = ((row_slot + turn) & 3) == lane_slot[:, : value.shape[1]]
        return jnp.where(match, value, 0.0).astype(BF16)

    for g in range(groups):
        first, second = 1 if g == 0 else 0, -1 if g == last else 0
        plain = upper(g, 0)
        high = mm(upper(g, first) if first else plain, spread)
        low = lower(g, second - 1)
        wf_ref[g, :LANES, :LANES] = fit(high[:, :LANES], first)
        wf_ref[g, :LANES, LANES:] = fit(high[:, LANES:wide], first + 1)
        wf_ref[g, LANES:, :LANES] = fit(low[0], second - 1)
        wf_ref[g, LANES:, LANES:] = fit(low[1], second)
        wk_ref[g, :LANES, :LANES] = fit(high[:, wide : 3 * LANES], first)
        wk_ref[g, :LANES, LANES:] = fit(high[:, 3 * LANES :], first + 1)
        wk_ref[g, LANES:, :LANES] = fit(mm_nt(spread_t, plain), second - 1)
        wk_ref[g, LANES:, LANES:] = fit(low[2], second)
        if first or second:
            if first:
                high = mm(plain, spread)
            if second:
                low = lower(g, -1)
            at = 0 if first else 1
            wa_ref[at, :LANES, :LANES] = fit(high[:, :LANES], -second)
            wa_ref[at, :LANES, LANES:] = fit(high[:, LANES:wide], 1 - first)
            wa_ref[at, LANES:, :LANES] = fit(low[0], -1 - second)
            wa_ref[at, LANES:, LANES:] = fit(low[1], -first)

    lane = lane_slot[:, :LANES]

    def choose(parts, shift):
        got = parts[0]
        for j in range(1, SLOTS):
            got = jnp.where(lane == (j + shift) % SLOTS, parts[j], got)
        return got

    forward, adjoint = [], []
    for g in range(groups):
        parts = [strip(g + groups * j, slice(chunk)).astype(F32) for j in range(SLOTS)]
        blocks = [choose(parts, i) for i in range(4)]
        forward.append(jnp.concatenate(blocks[:2], axis=1))
        halves = [pltpu.roll(v, 2 * edge, 1) for v in blocks[2:]]
        adjoint.append(jnp.concatenate(halves, axis=1))

    def up(parts, at):
        return [parts[-1]] + parts[:-1] if at == 1 else list(parts)

    def down(parts, at):
        return list(parts) if at == 1 else parts[1:] + [parts[0]]

    def arrive(parts, at, first_up):
        first, second = [v[:, :LANES] for v in parts], [v[:, LANES:] for v in parts]
        if first_up:
            first, second = up(first, at), down(second, at)
        else:
            first, second = down(first, at), up(second, at)
        return [jnp.concatenate([p, q], axis=1).astype(BF16) for p, q in zip(first, second)]

    def turned(parts, first_up):
        def turn(part, half, by):
            halves = [part[:, :LANES], part[:, LANES:]]
            halves[half] = pltpu.roll(halves[half].astype(F32), by, 1).astype(BF16)
            return jnp.concatenate(halves, axis=1)

        parts = list(parts)
        parts[0] = turn(parts[0], 0 if first_up else 1, edge)
        parts[last] = turn(parts[last], 1 if first_up else 0, LANES - edge)
        return parts

    def iterate(base, step, first_up):
        even, odd = [base[g] for g in evens], [base[g] for g in odds]
        ahead, behind = odd, even
        z = arrive(ahead, 1, first_up)
        ahead = [even[i] + step(z[i], g) for i, g in enumerate(evens)]
        for t in range(1, SWEEPS - 2):
            at = (t + 1) % 2
            z = arrive(ahead, at, first_up)
            y = arrive(behind, at, first_up)
            add = odd if at == 0 else even
            both = []
            for i, g in enumerate(odds if at == 0 else evens):
                both.append(step(jnp.concatenate([z[i], y[i]], axis=0), g))
            ahead = [add[i] + v[:chunk] for i, v in enumerate(both)]
            behind = [add[i] + v[chunk:] for i, v in enumerate(both)]
        at = (SWEEPS - 1) % 2
        y = arrive(behind, at, first_up)
        add = odd if at == 0 else even
        behind = [
            add[i] + step(y[i], g) for i, g in enumerate(odds if at == 0 else evens)
        ]
        gets_ahead, gets_behind = arrive(ahead, at, first_up), arrive(behind, 1 - at, first_up)
        got = [None] * groups
        for i, g in enumerate(odds if at == 0 else evens):
            got[g] = gets_ahead[i]
        for i, g in enumerate(evens if at == 0 else odds):
            got[g] = gets_behind[i]
        return got

    z = iterate(forward, lambda v, g: mm(v, wf_ref[g]), True)
    base = [adjoint[g] + mm(z[g], wk_ref[g]) for g in range(groups)]
    ends = {0: wa_ref.at[0], last: wa_ref.at[1]}
    y = iterate(base, lambda v, g: mm_nt(v, ends[g][...] if g in ends else wf_ref[g]), False)
    z, y = turned(z, True), turned(y, False)
    for i, g in enumerate(evens):
        own = [jnp.where(core == 0, v[g], v[g + 1]).astype(F32) for v in (y, z)]
        parts = [own[0][:, :LANES], own[0][:, LANES:]]
        parts += [pltpu.roll(own[1][:, v], 2 * edge, 1) for v in (slice(LANES), slice(LANES, wide))]
        for j in range(SLOTS):
            o_ref[(g + groups * j) // 2] = choose(parts, j).astype(BF16)


def finish(chips, scale_ref, p_ref, b_ref, l_ref, r_ref, zy_ref, o_ref):
    count, block, modes = b_ref.shape
    edge = l_ref.shape[0]
    couple = jnp.concatenate([l_ref[...], r_ref[...]], axis=0).astype(F32).T
    pick = (
        lax.broadcasted_iota(jnp.int32, (2 * edge, LANES), 0)
        == lax.broadcasted_iota(jnp.int32, (2 * edge, LANES), 1)
    ).astype(F32)
    front = jnp.concatenate([jnp.zeros_like(couple), couple], axis=1)
    front = jnp.concatenate([front, pick], axis=0)
    front = pltpu.roll(front, own_slot(chips) * edge, 1).astype(BF16)
    energies = range(count)
    got = [mm_nt(front, zy_ref[e]) for e in energies]
    rhs = [(b_ref[e].astype(F32) + got[e][:block]).astype(BF16) for e in energies]
    psi = [mm(p_ref[e], rhs[e]).astype(BF16) for e in energies]
    scale = [jnp.concatenate([scale_ref[e]] * (modes // LANES), axis=1) for e in energies]
    source = [psi[e].astype(F32) * scale[e] for e in energies]
    update = [
        jnp.concatenate(
            [
                source[e][:edge] + got[e][block + edge :],
                source[e][edge : block - edge],
                source[e][block - edge :] + got[e][block : block + edge],
            ],
            axis=0,
        ).astype(BF16)
        for e in energies
    ]
    total = jnp.zeros((block, block), F32)
    for e in energies:
        part = mm_nt(update[e], psi[e])
        high = part.astype(BF16)
        low = (part - high.astype(F32)).astype(BF16)
        inverse_t = p_ref[e].T
        total += mm(inverse_t, high) + mm(inverse_t, low)
    total = (total * (-1.0 / modes)).astype(BF16)
    pieces, owned, _ = o_ref.shape
    for k in range(pieces):
        o_ref[k] = total[k * owned : (k + 1) * owned]


SMEM = pl.BlockSpec(memory_space=pltpu.SMEM)
VMEM = pl.BlockSpec(memory_space=pltpu.VMEM)
ANY = pl.BlockSpec(memory_space=pltpu.HBM)
PARAMS = dict(compiler_params=pltpu.CompilerParams(vmem_limit_bytes=24 * 1024 * 1024))


shape = jax.ShapeDtypeStruct


def call_prepare(scalars, inverse, source, left, right, chips):
    count, block, modes = source.shape
    edge = left.shape[0]
    held = [pltpu.with_memory_space_constraint(scalars[0], pltpu.HBM)]
    tensors = [
        pltpu.with_memory_space_constraint(v, pltpu.HBM) for v in (inverse, source, left, right)
    ]
    pieces = (chips, count * modes // chips + edge + edge * 3 // 4, 4 * edge)
    return pl.pallas_call(
        prepare,
        out_shape=(pltpu.VMEM(pieces, BF16), pltpu.VMEM((count, block, LANES), F32)),
        in_specs=[ANY, SMEM, SMEM] + [ANY] * 4,
        out_specs=(VMEM, VMEM),
        scratch_shapes=[
            pltpu.SMEM((count,), F32),
            pltpu.VMEM((count, block, block), BF16),
            pltpu.VMEM((count, block, modes), BF16),
            pltpu.VMEM((2 * edge, block), BF16),
            pltpu.VMEM((count, 4 * edge, block), BF16),
            pltpu.SemaphoreType.DMA((5,)),
        ],
        name="prepare",
        **PARAMS,
    )(*held, *scalars[1:], *tensors)


def call_sweeps(given, chunk):
    cores, chips, _, lanes = given.shape
    weights = (cores * chips // SLOTS, 2 * LANES, 2 * LANES)
    return pl.pallas_call(
        sweep_all,
        out_shape=shape((chips, chunk, lanes), BF16),
        in_specs=[VMEM],
        out_specs=VMEM,
        scratch_shapes=[
            pltpu.VMEM(weights, BF16),
            pltpu.VMEM((2,) + weights[1:], BF16),
            pltpu.VMEM(weights, BF16),
        ],
        name="sweeps",
        **PARAMS,
    )(given)


def call_finish(scale, inverse, source, left, right, columns, energies, owned, chips):
    block = inverse.shape[1]
    return pl.pallas_call(
        functools.partial(finish, chips),
        out_shape=shape((energies, owned, block), BF16),
        in_specs=[VMEM] * 6,
        out_specs=VMEM,
        name="finish",
        **PARAMS,
    )(scale, inverse, source, left, right, columns)


def body(
    inverse_blocks,
    source,
    left_coupling,
    right_coupling,
    energy_weights,
    collector_low,
    collector_high,
):
    count, block, modes = source.shape
    edge = left_coupling.shape[0]
    chips = lax.axis_size("chip")
    energies = lax.axis_size("energy")
    chunk = count * modes // chips
    owned = block // energies
    scalars = (energy_weights, collector_low, collector_high)

    pieces, scale = call_prepare(
        scalars, inverse_blocks, source, left_coupling, right_coupling, chips
    )
    mine = lax.all_to_all(pieces, "chip", 0, 0, tiled=True)
    given = lax.all_gather(mine, "core")
    out = call_sweeps(given, chunk)
    out = lax.all_to_all(out, "chip", 0, 0, tiled=True)
    out = call_finish(
        scale,
        inverse_blocks,
        source,
        left_coupling,
        right_coupling,
        out.reshape(count, modes, 4 * edge),
        energies,
        owned,
        chips,
    )
    out = lax.all_to_all(out, "energy", 0, 0, tiled=True)
    return jnp.sum(out.astype(F32), axis=0)[None]


def solution(mesh):
    energies, strips = mesh.devices.shape
    cores = 2
    split = jax.sharding.Mesh(
        mesh.devices.reshape(energies, strips // cores, cores), ("energy", "chip", "core")
    )
    width = ("chip", "core")
    placed = (
        P("energy", width, None),
        P("energy", width, None),
        P(width, None),
        P(width, None),
        P("energy"),
        P(width),
        P(width),
    )
    return jax.shard_map(
        body, mesh=split, in_specs=placed, out_specs=P(width, "energy", None), check_vma=False
    )
```

```python
import functools

import jax
import jax.numpy as jnp
from jax import lax
from jax.experimental import pallas as pl
from jax.experimental.pallas import tpu as pltpu
from jax.sharding import PartitionSpec as P

SWEEPS = 10
LANES = 128
F32 = jnp.float32
BF16 = jnp.bfloat16


def mm(a, b):
    return jnp.dot(a, b, preferred_element_type=F32)


def mm_nt(a, b):
    return lax.dot_general(a, b, (((1,), (1,)), ((), ())), preferred_element_type=F32)


SLOTS = 4


def own_slot(chips):
    return lax.axis_index("chip") // (chips // SLOTS)


def pack(step, middle):
    edge = step.shape[0] // 2
    most = edge * 3 // 4
    low = [step[edge:, :edge], step[edge:, edge:], middle[edge:, edge:]]
    rest = jnp.concatenate([v[most:] for v in low], axis=0)
    return jnp.concatenate(
        [
            jnp.concatenate([step[:edge], middle[:edge]], axis=1),
            jnp.concatenate([v[:most] for v in low] + [rest], axis=1),
        ],
        axis=0,
    )


def prepare(
    w_hbm,
    low_ref,
    high_ref,
    p_hbm,
    b_hbm,
    l_hbm,
    r_hbm,
    o_ref,
    scale_ref,
    w_ref,
    p_ref,
    b_ref,
    c_ref,
    q_ref,
    sems,
):
    count, block, modes = b_ref.shape
    edge = l_hbm.shape[0]
    fetch = [
        (w_hbm, w_ref),
        (l_hbm, c_ref.at[pl.ds(0, edge)]),
        (r_hbm, c_ref.at[pl.ds(edge, edge)]),
        (p_hbm, p_ref),
        (b_hbm, b_ref),
    ]
    fetch = [pltpu.make_async_copy(*ends, sems.at[i]) for i, ends in enumerate(fetch)]
    for copy in fetch:
        copy.start()
    fetch[0].wait()
    low, high = low_ref[0], high_ref[0]
    at = lax.broadcasted_iota(jnp.int32, (block, LANES), 0)
    inside = (at >= low) & (at < high)
    for e in range(count):
        scale_ref[e] = jnp.where(inside, 2.0 * w_ref[e], 0.0)
    at = lax.broadcasted_iota(jnp.int32, (1, block), 1)
    inside = (at >= low) & (at < high)
    for copy in fetch[1:4]:
        copy.wait()
    couple = c_ref[...]
    each = o_ref.shape[0] // count
    chunk = modes // each
    energies = range(count)
    rim = [jnp.concatenate([p_ref[e, block - edge :], p_ref[e, :edge]], axis=0) for e in energies]
    u = [mm_nt(couple, p_ref[e]) for e in energies]
    step = [mm_nt(couple, rim[e]) for e in energies]
    weighted = [jnp.where(inside, u[e] * (2.0 * w_ref[e]), 0.0).astype(BF16) for e in energies]
    outer = [mm(weighted[e], p_ref[e]).astype(BF16) for e in energies]
    middle = [mm_nt(weighted[e], u[e].astype(BF16)) for e in energies]
    slot = own_slot(o_ref.shape[0])
    for e in energies:
        blocks = [rim[e][:edge], rim[e][edge:], outer[e][:edge], outer[e][edge:]]
        for i, rows in enumerate(blocks):
            at = pl.multiple_of(((slot + i) & 3) * edge, edge)
            q_ref[e, pl.ds(at, edge)] = rows
    fetch[4].wait()
    for e in energies:
        rows = mm(q_ref[e], b_ref[e])
        columns = rows.T.astype(BF16)
        exact = pack(step[e], middle[e])
        left = jnp.zeros_like(exact)
        for k in range(each):
            left += exact
            rounded = left.astype(BF16)
            left -= rounded.astype(F32)
            o_ref[e * each + k, chunk:] = rounded
            o_ref[e * each + k, :chunk] = columns[k * chunk : (k + 1) * chunk]


def sweep_all(x_ref, o_ref, wf_ref, wa_ref, wk_ref):
    chips, chunk, _ = o_ref.shape
    strips = chips * x_ref.shape[0]
    edge = LANES // SLOTS
    most = edge * 3 // 4
    groups = strips // SLOTS
    wide = 2 * LANES
    last = groups - 1
    core = lax.axis_index("core")
    skip = chunk
    evens, odds = range(0, groups, 2), range(1, groups, 2)

    def strip(s, rows):
        return x_ref[s % 2, s // 2, rows]

    at = lax.broadcasted_iota(jnp.int32, (1, 2 * wide), 1)
    source = ((at >> 7) << 5) | (at & 31)
    spread = lax.broadcasted_iota(jnp.int32, (LANES, 2 * wide), 0) == source
    spread = spread.astype(F32).astype(BF16)
    source = (lax.broadcasted_iota(jnp.int32, (LANES, 1), 0) & 31) | 96
    spread_t = lax.broadcasted_iota(jnp.int32, (LANES, LANES), 1) == source
    spread_t = spread_t.astype(F32).astype(BF16)
    row_slot = lax.broadcasted_iota(jnp.int32, (LANES, 1), 0) >> 5
    lane_slot = (lax.broadcasted_iota(jnp.int32, (1, wide), 1) >> 5) & 3

    def upper(g, turn):
        rows = slice(skip, skip + edge)
        return jnp.concatenate(
            [strip(g + groups * ((j + turn) % SLOTS), rows) for j in range(SLOTS)], axis=0
        )

    def lower(g, turn):
        rows = slice(skip + edge, skip + edge + most)
        short = [
            strip(g + groups * ((j + turn) % SLOTS), rows).astype(F32) for j in range(SLOTS)
        ]
        got = mm(jnp.concatenate(short, axis=0).astype(BF16), spread)
        parts = []
        for part in range(3):
            lanes = slice(part * LANES, (part + 1) * LANES)
            rows = []
            for j in range(SLOTS):
                rest = j * most + part * (edge - most)
                rows.append(got[j * most : (j + 1) * most, lanes])
                rows.append(got[rest : rest + edge - most, 3 * LANES :])
            parts.append(jnp.concatenate(rows, axis=0))
        return parts

    def fit(value, turn):
        match = ((row_slot + turn) & 3) == lane_slot[:, : value.shape[1]]
        return jnp.where(match, value, 0.0).astype(BF16)

    for g in range(groups):
        first, second = 1 if g == 0 else 0, -1 if g == last else 0
        plain = upper(g, 0)
        high = mm(upper(g, first) if first else plain, spread)
        low = lower(g, second - 1)
        wf_ref[g, :LANES, :LANES] = fit(high[:, :LANES], first)
        wf_ref[g, :LANES, LANES:] = fit(high[:, LANES:wide], first + 1)
        wf_ref[g, LANES:, :LANES] = fit(low[0], second - 1)
        wf_ref[g, LANES:, LANES:] = fit(low[1], second)
        wk_ref[g, :LANES, :LANES] = fit(high[:, wide : 3 * LANES], first)
        wk_ref[g, :LANES, LANES:] = fit(high[:, 3 * LANES :], first + 1)
        wk_ref[g, LANES:, :LANES] = fit(mm_nt(spread_t, plain), second - 1)
        wk_ref[g, LANES:, LANES:] = fit(low[2], second)
        if first or second:
            if first:
                high = mm(plain, spread)
            if second:
                low = lower(g, -1)
            at = 0 if first else 1
            wa_ref[at, :LANES, :LANES] = fit(high[:, :LANES], -second)
            wa_ref[at, :LANES, LANES:] = fit(high[:, LANES:wide], 1 - first)
            wa_ref[at, LANES:, :LANES] = fit(low[0], -1 - second)
            wa_ref[at, LANES:, LANES:] = fit(low[1], -first)

    lane = lane_slot[:, :LANES]

    def choose(parts, shift):
        got = parts[0]
        for j in range(1, SLOTS):
            got = jnp.where(lane == (j + shift) % SLOTS, parts[j], got)
        return got

    forward, adjoint = [], []
    for g in range(groups):
        parts = [strip(g + groups * j, slice(chunk)) for j in range(SLOTS)]
        blocks = [choose(parts, i).astype(F32) for i in range(4)]
        forward.append(jnp.concatenate(blocks[:2], axis=1))
        halves = [pltpu.roll(v, 2 * edge, 1) for v in blocks[2:]]
        adjoint.append(jnp.concatenate(halves, axis=1))

    def up(parts, at):
        return [parts[-1]] + parts[:-1] if at == 1 else list(parts)

    def down(parts, at):
        return list(parts) if at == 1 else parts[1:] + [parts[0]]

    def arrive(parts, at, first_up):
        first, second = [v[:, :LANES] for v in parts], [v[:, LANES:] for v in parts]
        if first_up:
            first, second = up(first, at), down(second, at)
        else:
            first, second = down(first, at), up(second, at)
        return [jnp.concatenate([p, q], axis=1).astype(BF16) for p, q in zip(first, second)]

    def turned(parts, first_up):
        def turn(part, half, by):
            halves = [part[:, :LANES], part[:, LANES:]]
            halves[half] = pltpu.roll(halves[half].astype(F32), by, 1).astype(BF16)
            return jnp.concatenate(halves, axis=1)

        parts = list(parts)
        parts[0] = turn(parts[0], 0 if first_up else 1, edge)
        parts[last] = turn(parts[last], 1 if first_up else 0, LANES - edge)
        return parts

    def iterate(base, step, first_up):
        even, odd = [base[g] for g in evens], [base[g] for g in odds]
        ahead, behind = odd, even
        z = arrive(ahead, 1, first_up)
        ahead = [even[i] + step(z[i], g) for i, g in enumerate(evens)]
        for t in range(1, SWEEPS - 2):
            at = (t + 1) % 2
            z = arrive(ahead, at, first_up)
            y = arrive(behind, at, first_up)
            add = odd if at == 0 else even
            both = []
            for i, g in enumerate(odds if at == 0 else evens):
                both.append(step(jnp.concatenate([z[i], y[i]], axis=0), g))
            ahead = [add[i] + v[:chunk] for i, v in enumerate(both)]
            behind = [add[i] + v[chunk:] for i, v in enumerate(both)]
        at = (SWEEPS - 1) % 2
        y = arrive(behind, at, first_up)
        add = odd if at == 0 else even
        behind = [
            add[i] + step(y[i], g) for i, g in enumerate(odds if at == 0 else evens)
        ]
        gets_ahead, gets_behind = arrive(ahead, at, first_up), arrive(behind, 1 - at, first_up)
        got = [None] * groups
        for i, g in enumerate(odds if at == 0 else evens):
            got[g] = gets_ahead[i]
        for i, g in enumerate(evens if at == 0 else odds):
            got[g] = gets_behind[i]
        return got

    z = iterate(forward, lambda v, g: mm(v, wf_ref[g]), True)
    base = [adjoint[g] + mm(z[g], wk_ref[g]) for g in range(groups)]
    ends = {0: wa_ref.at[0], last: wa_ref.at[1]}
    y = iterate(base, lambda v, g: mm_nt(v, ends[g][...] if g in ends else wf_ref[g]), False)
    z, y = turned(z, True), turned(y, False)
    for i, g in enumerate(evens):
        own = [jnp.where(core == 0, v[g], v[g + 1]).astype(F32) for v in (y, z)]
        parts = [own[0][:, :LANES], own[0][:, LANES:]]
        parts += [pltpu.roll(own[1][:, v], 2 * edge, 1) for v in (slice(LANES), slice(LANES, wide))]
        for j in range(SLOTS):
            o_ref[(g + groups * j) // 2] = choose(parts, j).astype(BF16)


def finish(chips, scale_ref, p_ref, b_ref, l_ref, r_ref, zy_ref, o_ref, front_ref):
    count, block, modes = b_ref.shape
    edge = l_ref.shape[0]
    slot = own_slot(chips)
    row = lax.broadcasted_iota(jnp.int32, (edge, LANES), 0)
    column = lax.broadcasted_iota(jnp.int32, (edge, LANES), 1)
    zero = jnp.zeros((edge, block), F32)
    rows = [
        jnp.concatenate([(column == row + i * edge).astype(F32), right], axis=1)
        for i, right in enumerate([zero, zero, l_ref[...].astype(F32), r_ref[...].astype(F32)])
    ]
    for i, value in enumerate(rows):
        if i > 1:
            value = jnp.where(lax.broadcasted_iota(jnp.int32, value.shape, 1) < LANES, 0.0, value)
        front_ref[pl.ds(pl.multiple_of(((slot + i) & 3) * edge, edge), edge)] = value
    front = front_ref[...].T.astype(BF16)
    energies = range(count)
    got = [mm_nt(front, zy_ref[e]) for e in energies]
    rhs = [(b_ref[e].astype(F32) + got[e][LANES:]).astype(BF16) for e in energies]
    psi = [mm(p_ref[e], rhs[e]).astype(BF16) for e in energies]
    scale = [jnp.concatenate([scale_ref[e]] * (modes // LANES), axis=1) for e in energies]
    source = [psi[e].astype(F32) * scale[e] for e in energies]
    update = [
        jnp.concatenate(
            [
                source[e][:edge] + got[e][edge : 2 * edge],
                source[e][edge : block - edge],
                source[e][block - edge :] + got[e][:edge],
            ],
            axis=0,
        ).astype(BF16)
        for e in energies
    ]
    total = jnp.zeros((block, block), F32)
    for e in energies:
        part = mm_nt(update[e], psi[e])
        high = part.astype(BF16)
        low = (part - high.astype(F32)).astype(BF16)
        inverse_t = p_ref[e].T
        total += mm(inverse_t, high) + mm(inverse_t, low)
    total = (total * (-1.0 / modes)).astype(BF16)
    pieces, owned, _ = o_ref.shape
    for k in range(pieces):
        o_ref[k] = total[k * owned : (k + 1) * owned]


SMEM = pl.BlockSpec(memory_space=pltpu.SMEM)
VMEM = pl.BlockSpec(memory_space=pltpu.VMEM)
ANY = pl.BlockSpec(memory_space=pltpu.HBM)
PARAMS = dict(compiler_params=pltpu.CompilerParams(vmem_limit_bytes=24 * 1024 * 1024))


shape = jax.ShapeDtypeStruct


def call_prepare(scalars, inverse, source, left, right, chips):
    count, block, modes = source.shape
    edge = left.shape[0]
    held = [pltpu.with_memory_space_constraint(scalars[0], pltpu.HBM)]
    tensors = [
        pltpu.with_memory_space_constraint(v, pltpu.HBM) for v in (inverse, source, left, right)
    ]
    pieces = (chips, count * modes // chips + edge + edge * 3 // 4, 4 * edge)
    return pl.pallas_call(
        prepare,
        out_shape=(pltpu.VMEM(pieces, BF16), pltpu.VMEM((count, block, LANES), F32)),
        in_specs=[ANY, SMEM, SMEM] + [ANY] * 4,
        out_specs=(VMEM, VMEM),
        scratch_shapes=[
            pltpu.SMEM((count,), F32),
            pltpu.VMEM((count, block, block), BF16),
            pltpu.VMEM((count, block, modes), BF16),
            pltpu.VMEM((2 * edge, block), BF16),
            pltpu.VMEM((count, 4 * edge, block), BF16),
            pltpu.SemaphoreType.DMA((5,)),
        ],
        name="prepare",
        **PARAMS,
    )(*held, *scalars[1:], *tensors)


def call_sweeps(given, chunk):
    cores, chips, _, lanes = given.shape
    weights = (cores * chips // SLOTS, 2 * LANES, 2 * LANES)
    return pl.pallas_call(
        sweep_all,
        out_shape=shape((chips, chunk, lanes), BF16),
        in_specs=[VMEM],
        out_specs=VMEM,
        scratch_shapes=[
            pltpu.VMEM(weights, BF16),
            pltpu.VMEM((2,) + weights[1:], BF16),
            pltpu.VMEM(weights, BF16),
        ],
        name="sweeps",
        **PARAMS,
    )(given)


def call_finish(scale, inverse, source, left, right, columns, energies, owned, chips):
    block = inverse.shape[1]
    return pl.pallas_call(
        functools.partial(finish, chips),
        out_shape=shape((energies, owned, block), BF16),
        in_specs=[VMEM] * 6,
        out_specs=VMEM,
        scratch_shapes=[pltpu.VMEM((LANES, LANES + block), F32)],
        name="finish",
        **PARAMS,
    )(scale, inverse, source, left, right, columns)


def body(
    inverse_blocks,
    source,
    left_coupling,
    right_coupling,
    energy_weights,
    collector_low,
    collector_high,
):
    count, block, modes = source.shape
    edge = left_coupling.shape[0]
    chips = lax.axis_size("chip")
    energies = lax.axis_size("energy")
    chunk = count * modes // chips
    owned = block // energies
    scalars = (energy_weights, collector_low, collector_high)

    pieces, scale = call_prepare(
        scalars, inverse_blocks, source, left_coupling, right_coupling, chips
    )
    mine = lax.all_to_all(pieces, "chip", 0, 0, tiled=True)
    given = lax.all_gather(mine, "core")
    out = call_sweeps(given, chunk)
    out = lax.all_to_all(out, "chip", 0, 0, tiled=True)
    out = call_finish(
        scale,
        inverse_blocks,
        source,
        left_coupling,
        right_coupling,
        out.reshape(count, modes, 4 * edge),
        energies,
        owned,
        chips,
    )
    out = lax.all_to_all(out, "energy", 0, 0, tiled=True)
    return jnp.sum(out.astype(F32), axis=0)[None]


def solution(mesh):
    energies, strips = mesh.devices.shape
    cores = 2
    split = jax.sharding.Mesh(
        mesh.devices.reshape(energies, strips // cores, cores), ("energy", "chip", "core")
    )
    width = ("chip", "core")
    placed = (
        P("energy", width, None),
        P("energy", width, None),
        P(width, None),
        P(width, None),
        P("energy"),
        P(width),
        P(width),
    )
    return jax.shard_map(
        body, mesh=split, in_specs=placed, out_specs=P(width, "energy", None), check_vma=False
    )
```

```python
import functools

import jax
import jax.numpy as jnp
from jax import lax
from jax.experimental import pallas as pl
from jax.experimental.pallas import tpu as pltpu
from jax.sharding import PartitionSpec as P

SWEEPS = 10
LANES = 128
F32 = jnp.float32
BF16 = jnp.bfloat16


def mm(a, b):
    return jnp.dot(a, b, preferred_element_type=F32)


def mm_nt(a, b):
    return lax.dot_general(a, b, (((1,), (1,)), ((), ())), preferred_element_type=F32)


SLOTS = 4


def own_slot(chips):
    return lax.axis_index("chip") // (chips // SLOTS)


def pack(step, middle):
    edge = step.shape[0] // 2
    most = edge * 3 // 4
    low = [step[edge:, :edge], step[edge:, edge:], middle[edge:, edge:]]
    rest = jnp.concatenate([v[most:] for v in low], axis=0)
    return jnp.concatenate(
        [
            jnp.concatenate([step[:edge], middle[:edge]], axis=1),
            jnp.concatenate([v[:most] for v in low] + [rest], axis=1),
        ],
        axis=0,
    )


def prepare(
    w_hbm,
    low_ref,
    high_ref,
    p_hbm,
    b_hbm,
    l_hbm,
    r_hbm,
    o_ref,
    scale_ref,
    front_ref,
    w_ref,
    p_ref,
    b_ref,
    c_ref,
    q_ref,
    f_ref,
    sems,
):
    count, block, modes = b_ref.shape
    edge = l_hbm.shape[0]
    fetch = [
        (w_hbm, w_ref),
        (l_hbm, c_ref.at[pl.ds(0, edge)]),
        (r_hbm, c_ref.at[pl.ds(edge, edge)]),
        (p_hbm, p_ref),
        (b_hbm, b_ref),
    ]
    fetch = [pltpu.make_async_copy(*ends, sems.at[i]) for i, ends in enumerate(fetch)]
    for copy in fetch:
        copy.start()
    fetch[0].wait()
    low, high = low_ref[0], high_ref[0]
    at = lax.broadcasted_iota(jnp.int32, (block, LANES), 0)
    inside = (at >= low) & (at < high)
    for e in range(count):
        scale_ref[e] = jnp.where(inside, 2.0 * w_ref[e], 0.0)
    at = lax.broadcasted_iota(jnp.int32, (1, block), 1)
    inside = (at >= low) & (at < high)
    fetch[1].wait()
    fetch[2].wait()
    slot = own_slot(o_ref.shape[0])
    row = lax.broadcasted_iota(jnp.int32, (edge, LANES), 0)
    column = lax.broadcasted_iota(jnp.int32, (edge, LANES), 1)
    zero = jnp.zeros((edge, block), F32)
    rows = [
        jnp.concatenate([(column == row + i * edge).astype(F32), right], axis=1)
        for i, right in enumerate([zero, zero, c_ref[:edge].astype(F32), c_ref[edge:].astype(F32)])
    ]
    for i, value in enumerate(rows):
        if i > 1:
            value = jnp.where(lax.broadcasted_iota(jnp.int32, value.shape, 1) < LANES, 0.0, value)
        f_ref[pl.ds(pl.multiple_of(((slot + i) & 3) * edge, edge), edge)] = value
    front_ref[...] = f_ref[...].T.astype(BF16)
    fetch[3].wait()
    couple = c_ref[...]
    each = o_ref.shape[0] // count
    chunk = modes // each
    energies = range(count)
    rim = [jnp.concatenate([p_ref[e, block - edge :], p_ref[e, :edge]], axis=0) for e in energies]
    u = [mm_nt(couple, p_ref[e]) for e in energies]
    step = [mm_nt(couple, rim[e]) for e in energies]
    weighted = [jnp.where(inside, u[e] * (2.0 * w_ref[e]), 0.0).astype(BF16) for e in energies]
    outer = [mm(weighted[e], p_ref[e]).astype(BF16) for e in energies]
    middle = [mm_nt(weighted[e], u[e].astype(BF16)) for e in energies]
    for e in energies:
        blocks = [rim[e][:edge], rim[e][edge:], outer[e][:edge], outer[e][edge:]]
        for i, rows in enumerate(blocks):
            at = pl.multiple_of(((slot + i) & 3) * edge, edge)
            q_ref[e, pl.ds(at, edge)] = rows
    fetch[4].wait()
    for e in energies:
        rows = mm(q_ref[e], b_ref[e])
        columns = rows.T.astype(BF16)
        exact = pack(step[e], middle[e])
        left = jnp.zeros_like(exact)
        for k in range(each):
            left += exact
            rounded = left.astype(BF16)
            left -= rounded.astype(F32)
            o_ref[e * each + k, chunk:] = rounded
            o_ref[e * each + k, :chunk] = columns[k * chunk : (k + 1) * chunk]


def sweep_all(x_ref, o_ref, wf_ref, wa_ref, wk_ref):
    chips, chunk, _ = o_ref.shape
    strips = chips * x_ref.shape[0]
    edge = LANES // SLOTS
    most = edge * 3 // 4
    groups = strips // SLOTS
    wide = 2 * LANES
    last = groups - 1
    core = lax.axis_index("core")
    skip = chunk
    evens, odds = range(0, groups, 2), range(1, groups, 2)

    def strip(s, rows):
        return x_ref[s % 2, s // 2, rows]

    at = lax.broadcasted_iota(jnp.int32, (1, 2 * wide), 1)
    source = ((at >> 7) << 5) | (at & 31)
    spread = lax.broadcasted_iota(jnp.int32, (LANES, 2 * wide), 0) == source
    spread = spread.astype(F32).astype(BF16)
    source = (lax.broadcasted_iota(jnp.int32, (LANES, 1), 0) & 31) | 96
    spread_t = lax.broadcasted_iota(jnp.int32, (LANES, LANES), 1) == source
    spread_t = spread_t.astype(F32).astype(BF16)
    row_slot = lax.broadcasted_iota(jnp.int32, (LANES, 1), 0) >> 5
    lane_slot = (lax.broadcasted_iota(jnp.int32, (1, wide), 1) >> 5) & 3

    def upper(g, turn):
        rows = slice(skip, skip + edge)
        return jnp.concatenate(
            [strip(g + groups * ((j + turn) % SLOTS), rows) for j in range(SLOTS)], axis=0
        )

    def lower(g, turn):
        rows = slice(skip + edge, skip + edge + most)
        short = [
            strip(g + groups * ((j + turn) % SLOTS), rows).astype(F32) for j in range(SLOTS)
        ]
        got = mm(jnp.concatenate(short, axis=0).astype(BF16), spread)
        parts = []
        for part in range(3):
            lanes = slice(part * LANES, (part + 1) * LANES)
            rows = []
            for j in range(SLOTS):
                rest = j * most + part * (edge - most)
                rows.append(got[j * most : (j + 1) * most, lanes])
                rows.append(got[rest : rest + edge - most, 3 * LANES :])
            parts.append(jnp.concatenate(rows, axis=0))
        return parts

    def fit(value, turn):
        match = ((row_slot + turn) & 3) == lane_slot[:, : value.shape[1]]
        return jnp.where(match, value, 0.0).astype(BF16)

    for g in range(groups):
        first, second = 1 if g == 0 else 0, -1 if g == last else 0
        plain = upper(g, 0)
        high = mm(upper(g, first) if first else plain, spread)
        low = lower(g, second - 1)
        wf_ref[g, :LANES, :LANES] = fit(high[:, :LANES], first)
        wf_ref[g, :LANES, LANES:] = fit(high[:, LANES:wide], first + 1)
        wf_ref[g, LANES:, :LANES] = fit(low[0], second - 1)
        wf_ref[g, LANES:, LANES:] = fit(low[1], second)
        wk_ref[g, :LANES, :LANES] = fit(high[:, wide : 3 * LANES], first)
        wk_ref[g, :LANES, LANES:] = fit(high[:, 3 * LANES :], first + 1)
        wk_ref[g, LANES:, :LANES] = fit(mm_nt(spread_t, plain), second - 1)
        wk_ref[g, LANES:, LANES:] = fit(low[2], second)
        if first or second:
            if first:
                high = mm(plain, spread)
            if second:
                low = lower(g, -1)
            at = 0 if first else 1
            wa_ref[at, :LANES, :LANES] = fit(high[:, :LANES], -second)
            wa_ref[at, :LANES, LANES:] = fit(high[:, LANES:wide], 1 - first)
            wa_ref[at, LANES:, :LANES] = fit(low[0], -1 - second)
            wa_ref[at, LANES:, LANES:] = fit(low[1], -first)

    lane = lane_slot[:, :LANES]

    def choose(parts, shift):
        got = parts[0]
        for j in range(1, SLOTS):
            got = jnp.where(lane == (j + shift) % SLOTS, parts[j], got)
        return got

    forward, adjoint = [], []
    for g in range(groups):
        parts = [strip(g + groups * j, slice(chunk)) for j in range(SLOTS)]
        blocks = [choose(parts, i).astype(F32) for i in range(4)]
        forward.append(jnp.concatenate(blocks[:2], axis=1))
        halves = [pltpu.roll(v, 2 * edge, 1) for v in blocks[2:]]
        adjoint.append(jnp.concatenate(halves, axis=1))

    def up(parts, at):
        return [parts[-1]] + parts[:-1] if at == 1 else list(parts)

    def down(parts, at):
        return list(parts) if at == 1 else parts[1:] + [parts[0]]

    def arrive(parts, at, first_up):
        first, second = [v[:, :LANES] for v in parts], [v[:, LANES:] for v in parts]
        if first_up:
            first, second = up(first, at), down(second, at)
        else:
            first, second = down(first, at), up(second, at)
        return [jnp.concatenate([p, q], axis=1).astype(BF16) for p, q in zip(first, second)]

    def turned(parts, first_up):
        def turn(part, half, by):
            halves = [part[:, :LANES], part[:, LANES:]]
            halves[half] = pltpu.roll(halves[half].astype(F32), by, 1).astype(BF16)
            return jnp.concatenate(halves, axis=1)

        parts = list(parts)
        parts[0] = turn(parts[0], 0 if first_up else 1, edge)
        parts[last] = turn(parts[last], 1 if first_up else 0, LANES - edge)
        return parts

    def iterate(base, step, first_up):
        even, odd = [base[g] for g in evens], [base[g] for g in odds]
        ahead, behind = odd, even
        z = arrive(ahead, 1, first_up)
        ahead = [even[i] + step(z[i], g) for i, g in enumerate(evens)]
        for t in range(1, SWEEPS - 2):
            at = (t + 1) % 2
            z = arrive(ahead, at, first_up)
            y = arrive(behind, at, first_up)
            add = odd if at == 0 else even
            both = []
            for i, g in enumerate(odds if at == 0 else evens):
                both.append(step(jnp.concatenate([z[i], y[i]], axis=0), g))
            ahead = [add[i] + v[:chunk] for i, v in enumerate(both)]
            behind = [add[i] + v[chunk:] for i, v in enumerate(both)]
        at = (SWEEPS - 1) % 2
        y = arrive(behind, at, first_up)
        add = odd if at == 0 else even
        behind = [
            add[i] + step(y[i], g) for i, g in enumerate(odds if at == 0 else evens)
        ]
        gets_ahead, gets_behind = arrive(ahead, at, first_up), arrive(behind, 1 - at, first_up)
        got = [None] * groups
        for i, g in enumerate(odds if at == 0 else evens):
            got[g] = gets_ahead[i]
        for i, g in enumerate(evens if at == 0 else odds):
            got[g] = gets_behind[i]
        return got

    z = iterate(forward, lambda v, g: mm(v, wf_ref[g]), True)
    base = [adjoint[g] + mm(z[g], wk_ref[g]) for g in range(groups)]
    ends = {0: wa_ref.at[0], last: wa_ref.at[1]}
    y = iterate(base, lambda v, g: mm_nt(v, ends[g][...] if g in ends else wf_ref[g]), False)
    z, y = turned(z, True), turned(y, False)
    for i, g in enumerate(evens):
        own = [jnp.where(core == 0, v[g], v[g + 1]).astype(F32) for v in (y, z)]
        parts = [own[0][:, :LANES], own[0][:, LANES:]]
        parts += [pltpu.roll(own[1][:, v], 2 * edge, 1) for v in (slice(LANES), slice(LANES, wide))]
        for j in range(SLOTS):
            o_ref[(g + groups * j) // 2] = choose(parts, j).astype(BF16)


def finish(edge, scale_ref, front_ref, p_ref, b_ref, zy_ref, o_ref):
    count, block, modes = b_ref.shape
    energies = range(count)
    got = [mm_nt(front_ref[...], zy_ref[e]) for e in energies]
    rhs = [(b_ref[e].astype(F32) + got[e][LANES:]).astype(BF16) for e in energies]
    psi = [mm(p_ref[e], rhs[e]).astype(BF16) for e in energies]
    scale = [jnp.concatenate([scale_ref[e]] * (modes // LANES), axis=1) for e in energies]
    source = [psi[e].astype(F32) * scale[e] for e in energies]
    update = [
        jnp.concatenate(
            [
                source[e][:edge] + got[e][edge : 2 * edge],
                source[e][edge : block - edge],
                source[e][block - edge :] + got[e][:edge],
            ],
            axis=0,
        ).astype(BF16)
        for e in energies
    ]
    total = jnp.zeros((block, block), F32)
    for e in energies:
        part = mm_nt(update[e], psi[e])
        high = part.astype(BF16)
        low = (part - high.astype(F32)).astype(BF16)
        inverse_t = p_ref[e].T
        total += mm(inverse_t, high) + mm(inverse_t, low)
    total = (total * (-1.0 / modes)).astype(BF16)
    pieces, owned, _ = o_ref.shape
    for k in range(pieces):
        o_ref[k] = total[k * owned : (k + 1) * owned]


SMEM = pl.BlockSpec(memory_space=pltpu.SMEM)
VMEM = pl.BlockSpec(memory_space=pltpu.VMEM)
ANY = pl.BlockSpec(memory_space=pltpu.HBM)
PARAMS = dict(compiler_params=pltpu.CompilerParams(vmem_limit_bytes=24 * 1024 * 1024))


shape = jax.ShapeDtypeStruct


def call_prepare(scalars, inverse, source, left, right, chips):
    count, block, modes = source.shape
    edge = left.shape[0]
    held = [pltpu.with_memory_space_constraint(scalars[0], pltpu.HBM)]
    tensors = [
        pltpu.with_memory_space_constraint(v, pltpu.HBM) for v in (inverse, source, left, right)
    ]
    pieces = (chips, count * modes // chips + edge + edge * 3 // 4, 4 * edge)
    return pl.pallas_call(
        prepare,
        out_shape=(
            pltpu.VMEM(pieces, BF16),
            pltpu.VMEM((count, block, LANES), F32),
            pltpu.VMEM((LANES + block, LANES), BF16),
        ),
        in_specs=[ANY, SMEM, SMEM] + [ANY] * 4,
        out_specs=(VMEM, VMEM, VMEM),
        scratch_shapes=[
            pltpu.SMEM((count,), F32),
            pltpu.VMEM((count, block, block), BF16),
            pltpu.VMEM((count, block, modes), BF16),
            pltpu.VMEM((2 * edge, block), BF16),
            pltpu.VMEM((count, 4 * edge, block), BF16),
            pltpu.VMEM((LANES, LANES + block), F32),
            pltpu.SemaphoreType.DMA((5,)),
        ],
        name="prepare",
        **PARAMS,
    )(*held, *scalars[1:], *tensors)


def call_sweeps(given, chunk):
    cores, chips, _, lanes = given.shape
    weights = (cores * chips // SLOTS, 2 * LANES, 2 * LANES)
    return pl.pallas_call(
        sweep_all,
        out_shape=shape((chips, chunk, lanes), BF16),
        in_specs=[VMEM],
        out_specs=VMEM,
        scratch_shapes=[
            pltpu.VMEM(weights, BF16),
            pltpu.VMEM((2,) + weights[1:], BF16),
            pltpu.VMEM(weights, BF16),
        ],
        name="sweeps",
        **PARAMS,
    )(given)


def call_finish(scale, front, inverse, source, columns, energies, owned):
    block = inverse.shape[1]
    return pl.pallas_call(
        functools.partial(finish, columns.shape[2] // 4),
        out_shape=shape((energies, owned, block), BF16),
        in_specs=[VMEM] * 5,
        out_specs=VMEM,
        name="finish",
        **PARAMS,
    )(scale, front, inverse, source, columns)


def body(
    inverse_blocks,
    source,
    left_coupling,
    right_coupling,
    energy_weights,
    collector_low,
    collector_high,
):
    count, block, modes = source.shape
    edge = left_coupling.shape[0]
    chips = lax.axis_size("chip")
    energies = lax.axis_size("energy")
    chunk = count * modes // chips
    owned = block // energies
    scalars = (energy_weights, collector_low, collector_high)

    pieces, scale, front = call_prepare(
        scalars, inverse_blocks, source, left_coupling, right_coupling, chips
    )
    mine = lax.all_to_all(pieces, "chip", 0, 0, tiled=True)
    given = lax.all_gather(mine, "core")
    out = call_sweeps(given, chunk)
    out = lax.all_to_all(out, "chip", 0, 0, tiled=True)
    out = call_finish(
        scale,
        front,
        inverse_blocks,
        source,
        out.reshape(count, modes, 4 * edge),
        energies,
        owned,
    )
    out = lax.all_to_all(out, "energy", 0, 0, tiled=True)
    return jnp.sum(out.astype(F32), axis=0)[None]


def solution(mesh):
    energies, strips = mesh.devices.shape
    cores = 2
    split = jax.sharding.Mesh(
        mesh.devices.reshape(energies, strips // cores, cores), ("energy", "chip", "core")
    )
    width = ("chip", "core")
    placed = (
        P("energy", width, None),
        P("energy", width, None),
        P(width, None),
        P(width, None),
        P("energy"),
        P(width),
        P(width),
    )
    return jax.shard_map(
        body, mesh=split, in_specs=placed, out_specs=P(width, "energy", None), check_vma=False
    )
```

```python
import functools

import jax
import jax.numpy as jnp
from jax import lax
from jax.experimental import pallas as pl
from jax.experimental.pallas import tpu as pltpu
from jax.sharding import PartitionSpec as P

SWEEPS = 10
LANES = 128
F32 = jnp.float32
BF16 = jnp.bfloat16


def mm(a, b):
    return jnp.dot(a, b, preferred_element_type=F32)


def mm_nt(a, b):
    return lax.dot_general(a, b, (((1,), (1,)), ((), ())), preferred_element_type=F32)


SLOTS = 4


def own_slot(chips):
    return lax.axis_index("chip") // (chips // SLOTS)


def pack(step, middle):
    edge = step.shape[0] // 2
    most = edge * 3 // 4
    low = [step[edge:, :edge], step[edge:, edge:], middle[edge:, edge:]]
    rest = jnp.concatenate([v[most:] for v in low], axis=0)
    return jnp.concatenate(
        [
            jnp.concatenate([step[:edge], middle[:edge]], axis=1),
            jnp.concatenate([v[:most] for v in low] + [rest], axis=1),
        ],
        axis=0,
    )


def prepare(
    w_hbm,
    low_ref,
    high_ref,
    p_hbm,
    b_hbm,
    l_hbm,
    r_hbm,
    o_ref,
    scale_ref,
    front_ref,
    w_ref,
    p_ref,
    b_ref,
    c_ref,
    q_ref,
    f_ref,
    sems,
):
    count, block, modes = b_ref.shape
    edge = l_hbm.shape[0]
    fetch = [
        (w_hbm, w_ref),
        (l_hbm, c_ref.at[pl.ds(0, edge)]),
        (r_hbm, c_ref.at[pl.ds(edge, edge)]),
        (p_hbm, p_ref),
        (b_hbm, b_ref),
    ]
    fetch = [pltpu.make_async_copy(*ends, sems.at[i]) for i, ends in enumerate(fetch)]
    for i in (3, 1, 2, 0, 4):
        fetch[i].start()
    fetch[0].wait()
    low, high = low_ref[0], high_ref[0]
    at = lax.broadcasted_iota(jnp.int32, (block, LANES), 0)
    inside = (at >= low) & (at < high)
    for e in range(count):
        scale_ref[e] = jnp.where(inside, 2.0 * w_ref[e], 0.0)
    at = lax.broadcasted_iota(jnp.int32, (1, block), 1)
    inside = (at >= low) & (at < high)
    fetch[1].wait()
    fetch[2].wait()
    slot = own_slot(o_ref.shape[0])
    row = lax.broadcasted_iota(jnp.int32, (edge, LANES), 0)
    column = lax.broadcasted_iota(jnp.int32, (edge, LANES), 1)
    zero = jnp.zeros((edge, block), F32)
    rows = [
        jnp.concatenate([(column == row + i * edge).astype(F32), right], axis=1)
        for i, right in enumerate([zero, zero, c_ref[:edge].astype(F32), c_ref[edge:].astype(F32)])
    ]
    for i, value in enumerate(rows):
        if i > 1:
            value = jnp.where(lax.broadcasted_iota(jnp.int32, value.shape, 1) < LANES, 0.0, value)
        f_ref[pl.ds(pl.multiple_of(((slot + i) & 3) * edge, edge), edge)] = value
    front_ref[...] = f_ref[...].T.astype(BF16)
    fetch[3].wait()
    couple = c_ref[...]
    each = o_ref.shape[0] // count
    chunk = modes // each
    energies = range(count)
    rim = [jnp.concatenate([p_ref[e, block - edge :], p_ref[e, :edge]], axis=0) for e in energies]
    u = [mm_nt(couple, p_ref[e]) for e in energies]
    step = [mm_nt(couple, rim[e]) for e in energies]
    weighted = [jnp.where(inside, u[e] * (2.0 * w_ref[e]), 0.0).astype(BF16) for e in energies]
    outer = [mm(weighted[e], p_ref[e]).astype(BF16) for e in energies]
    middle = [mm_nt(weighted[e], u[e].astype(BF16)) for e in energies]
    for e in energies:
        blocks = [rim[e][:edge], rim[e][edge:], outer[e][:edge], outer[e][edge:]]
        for i, rows in enumerate(blocks):
            at = pl.multiple_of(((slot + i) & 3) * edge, edge)
            q_ref[e, pl.ds(at, edge)] = rows
    fetch[4].wait()
    for e in energies:
        rows = mm(q_ref[e], b_ref[e])
        columns = rows.T.astype(BF16)
        exact = pack(step[e], middle[e])
        left = jnp.zeros_like(exact)
        for k in range(each):
            left += exact
            rounded = left.astype(BF16)
            left -= rounded.astype(F32)
            o_ref[e * each + k, chunk:] = rounded
            o_ref[e * each + k, :chunk] = columns[k * chunk : (k + 1) * chunk]


def sweep_all(x_ref, o_ref, wf_ref, wa_ref, wk_ref):
    chips, chunk, _ = o_ref.shape
    strips = chips * x_ref.shape[0]
    edge = LANES // SLOTS
    most = edge * 3 // 4
    groups = strips // SLOTS
    wide = 2 * LANES
    last = groups - 1
    core = lax.axis_index("core")
    skip = chunk
    evens, odds = range(0, groups, 2), range(1, groups, 2)

    def strip(s, rows):
        return x_ref[s % 2, s // 2, rows]

    at = lax.broadcasted_iota(jnp.int32, (1, 2 * wide), 1)
    source = ((at >> 7) << 5) | (at & 31)
    spread = lax.broadcasted_iota(jnp.int32, (LANES, 2 * wide), 0) == source
    spread = spread.astype(F32).astype(BF16)
    source = (lax.broadcasted_iota(jnp.int32, (LANES, 1), 0) & 31) | 96
    spread_t = lax.broadcasted_iota(jnp.int32, (LANES, LANES), 1) == source
    spread_t = spread_t.astype(F32).astype(BF16)
    row_slot = lax.broadcasted_iota(jnp.int32, (LANES, 1), 0) >> 5
    lane_slot = (lax.broadcasted_iota(jnp.int32, (1, wide), 1) >> 5) & 3

    def upper(g, turn):
        rows = slice(skip, skip + edge)
        return jnp.concatenate(
            [strip(g + groups * ((j + turn) % SLOTS), rows) for j in range(SLOTS)], axis=0
        )

    def lower(g, turn):
        rows = slice(skip + edge, skip + edge + most)
        short = [
            strip(g + groups * ((j + turn) % SLOTS), rows).astype(F32) for j in range(SLOTS)
        ]
        got = mm(jnp.concatenate(short, axis=0).astype(BF16), spread)
        parts = []
        for part in range(3):
            lanes = slice(part * LANES, (part + 1) * LANES)
            rows = []
            for j in range(SLOTS):
                rest = j * most + part * (edge - most)
                rows.append(got[j * most : (j + 1) * most, lanes])
                rows.append(got[rest : rest + edge - most, 3 * LANES :])
            parts.append(jnp.concatenate(rows, axis=0))
        return parts

    def fit(value, turn):
        match = ((row_slot + turn) & 3) == lane_slot[:, : value.shape[1]]
        return jnp.where(match, value, 0.0).astype(BF16)

    for g in range(groups):
        first, second = 1 if g == 0 else 0, -1 if g == last else 0
        plain = upper(g, 0)
        high = mm(upper(g, first) if first else plain, spread)
        low = lower(g, second - 1)
        wf_ref[g, :LANES, :LANES] = fit(high[:, :LANES], first)
        wf_ref[g, :LANES, LANES:] = fit(high[:, LANES:wide], first + 1)
        wf_ref[g, LANES:, :LANES] = fit(low[0], second - 1)
        wf_ref[g, LANES:, LANES:] = fit(low[1], second)
        wk_ref[g, :LANES, :LANES] = fit(high[:, wide : 3 * LANES], first)
        wk_ref[g, :LANES, LANES:] = fit(high[:, 3 * LANES :], first + 1)
        wk_ref[g, LANES:, :LANES] = fit(mm_nt(spread_t, plain), second - 1)
        wk_ref[g, LANES:, LANES:] = fit(low[2], second)
        if first or second:
            if first:
                high = mm(plain, spread)
            if second:
                low = lower(g, -1)
            at = 0 if first else 1
            wa_ref[at, :LANES, :LANES] = fit(high[:, :LANES], -second)
            wa_ref[at, :LANES, LANES:] = fit(high[:, LANES:wide], 1 - first)
            wa_ref[at, LANES:, :LANES] = fit(low[0], -1 - second)
            wa_ref[at, LANES:, LANES:] = fit(low[1], -first)

    lane = lane_slot[:, :LANES]

    def choose(parts, shift):
        got = parts[0]
        for j in range(1, SLOTS):
            got = jnp.where(lane == (j + shift) % SLOTS, parts[j], got)
        return got

    forward, adjoint = [], []
    for g in range(groups):
        parts = [strip(g + groups * j, slice(chunk)) for j in range(SLOTS)]
        blocks = [choose(parts, i).astype(F32) for i in range(4)]
        forward.append(jnp.concatenate(blocks[:2], axis=1))
        halves = [pltpu.roll(v, 2 * edge, 1) for v in blocks[2:]]
        adjoint.append(jnp.concatenate(halves, axis=1))

    def up(parts, at):
        return [parts[-1]] + parts[:-1] if at == 1 else list(parts)

    def down(parts, at):
        return list(parts) if at == 1 else parts[1:] + [parts[0]]

    def arrive(parts, at, first_up):
        first, second = [v[:, :LANES] for v in parts], [v[:, LANES:] for v in parts]
        if first_up:
            first, second = up(first, at), down(second, at)
        else:
            first, second = down(first, at), up(second, at)
        return [jnp.concatenate([p, q], axis=1).astype(BF16) for p, q in zip(first, second)]

    def turned(parts, first_up):
        def turn(part, half, by):
            halves = [part[:, :LANES], part[:, LANES:]]
            halves[half] = pltpu.roll(halves[half].astype(F32), by, 1).astype(BF16)
            return jnp.concatenate(halves, axis=1)

        parts = list(parts)
        parts[0] = turn(parts[0], 0 if first_up else 1, edge)
        parts[last] = turn(parts[last], 1 if first_up else 0, LANES - edge)
        return parts

    def iterate(base, step, first_up):
        even, odd = [base[g] for g in evens], [base[g] for g in odds]
        ahead, behind = odd, even
        z = arrive(ahead, 1, first_up)
        ahead = [even[i] + step(z[i], g) for i, g in enumerate(evens)]
        for t in range(1, SWEEPS - 2):
            at = (t + 1) % 2
            z = arrive(ahead, at, first_up)
            y = arrive(behind, at, first_up)
            add = odd if at == 0 else even
            both = []
            for i, g in enumerate(odds if at == 0 else evens):
                both.append(step(jnp.concatenate([z[i], y[i]], axis=0), g))
            ahead = [add[i] + v[:chunk] for i, v in enumerate(both)]
            behind = [add[i] + v[chunk:] for i, v in enumerate(both)]
        at = (SWEEPS - 1) % 2
        y = arrive(behind, at, first_up)
        add = odd if at == 0 else even
        behind = [
            add[i] + step(y[i], g) for i, g in enumerate(odds if at == 0 else evens)
        ]
        gets_ahead, gets_behind = arrive(ahead, at, first_up), arrive(behind, 1 - at, first_up)
        got = [None] * groups
        for i, g in enumerate(odds if at == 0 else evens):
            got[g] = gets_ahead[i]
        for i, g in enumerate(evens if at == 0 else odds):
            got[g] = gets_behind[i]
        return got

    z = iterate(forward, lambda v, g: mm(v, wf_ref[g]), True)
    base = [adjoint[g] + mm(z[g], wk_ref[g]) for g in range(groups)]
    ends = {0: wa_ref.at[0], last: wa_ref.at[1]}
    y = iterate(base, lambda v, g: mm_nt(v, ends[g][...] if g in ends else wf_ref[g]), False)
    z, y = turned(z, True), turned(y, False)
    for i, g in enumerate(evens):
        own = [jnp.where(core == 0, v[g], v[g + 1]).astype(F32) for v in (y, z)]
        parts = [own[0][:, :LANES], own[0][:, LANES:]]
        parts += [pltpu.roll(own[1][:, v], 2 * edge, 1) for v in (slice(LANES), slice(LANES, wide))]
        for j in range(SLOTS):
            o_ref[(g + groups * j) // 2] = choose(parts, j).astype(BF16)


def finish(edge, scale_ref, front_ref, p_ref, b_ref, zy_ref, o_ref):
    count, block, modes = b_ref.shape
    energies = range(count)
    got = [mm_nt(front_ref[...], zy_ref[e]) for e in energies]
    rhs = [(b_ref[e].astype(F32) + got[e][LANES:]).astype(BF16) for e in energies]
    psi = [mm(p_ref[e], rhs[e]).astype(BF16) for e in energies]
    scale = [jnp.concatenate([scale_ref[e]] * (modes // LANES), axis=1) for e in energies]
    source = [psi[e].astype(F32) * scale[e] for e in energies]
    update = [
        jnp.concatenate(
            [
                source[e][:edge] + got[e][edge : 2 * edge],
                source[e][edge : block - edge],
                source[e][block - edge :] + got[e][:edge],
            ],
            axis=0,
        ).astype(BF16)
        for e in energies
    ]
    total = jnp.zeros((block, block), F32)
    for e in energies:
        part = mm_nt(update[e], psi[e])
        high = part.astype(BF16)
        low = (part - high.astype(F32)).astype(BF16)
        inverse_t = p_ref[e].T
        total += mm(inverse_t, high) + mm(inverse_t, low)
    total = (total * (-1.0 / modes)).astype(BF16)
    pieces, owned, _ = o_ref.shape
    for k in range(pieces):
        o_ref[k] = total[k * owned : (k + 1) * owned]


SMEM = pl.BlockSpec(memory_space=pltpu.SMEM)
VMEM = pl.BlockSpec(memory_space=pltpu.VMEM)
ANY = pl.BlockSpec(memory_space=pltpu.HBM)
PARAMS = dict(compiler_params=pltpu.CompilerParams(vmem_limit_bytes=24 * 1024 * 1024))


shape = jax.ShapeDtypeStruct


def call_prepare(scalars, inverse, source, left, right, chips):
    count, block, modes = source.shape
    edge = left.shape[0]
    held = [pltpu.with_memory_space_constraint(scalars[0], pltpu.HBM)]
    tensors = [
        pltpu.with_memory_space_constraint(v, pltpu.HBM) for v in (inverse, source, left, right)
    ]
    pieces = (chips, count * modes // chips + edge + edge * 3 // 4, 4 * edge)
    return pl.pallas_call(
        prepare,
        out_shape=(
            pltpu.VMEM(pieces, BF16),
            pltpu.VMEM((count, block, LANES), F32),
            pltpu.VMEM((LANES + block, LANES), BF16),
        ),
        in_specs=[ANY, SMEM, SMEM] + [ANY] * 4,
        out_specs=(VMEM, VMEM, VMEM),
        scratch_shapes=[
            pltpu.SMEM((count,), F32),
            pltpu.VMEM((count, block, block), BF16),
            pltpu.VMEM((count, block, modes), BF16),
            pltpu.VMEM((2 * edge, block), BF16),
            pltpu.VMEM((count, 4 * edge, block), BF16),
            pltpu.VMEM((LANES, LANES + block), F32),
            pltpu.SemaphoreType.DMA((5,)),
        ],
        name="prepare",
        **PARAMS,
    )(*held, *scalars[1:], *tensors)


def call_sweeps(given, chunk):
    cores, chips, _, lanes = given.shape
    weights = (cores * chips // SLOTS, 2 * LANES, 2 * LANES)
    return pl.pallas_call(
        sweep_all,
        out_shape=shape((chips, chunk, lanes), BF16),
        in_specs=[VMEM],
        out_specs=VMEM,
        scratch_shapes=[
            pltpu.VMEM(weights, BF16),
            pltpu.VMEM((2,) + weights[1:], BF16),
            pltpu.VMEM(weights, BF16),
        ],
        name="sweeps",
        **PARAMS,
    )(given)


def call_finish(scale, front, inverse, source, columns, energies, owned):
    block = inverse.shape[1]
    return pl.pallas_call(
        functools.partial(finish, columns.shape[2] // 4),
        out_shape=shape((energies, owned, block), BF16),
        in_specs=[VMEM] * 5,
        out_specs=VMEM,
        name="finish",
        **PARAMS,
    )(scale, front, inverse, source, columns)


def body(
    inverse_blocks,
    source,
    left_coupling,
    right_coupling,
    energy_weights,
    collector_low,
    collector_high,
):
    count, block, modes = source.shape
    edge = left_coupling.shape[0]
    chips = lax.axis_size("chip")
    energies = lax.axis_size("energy")
    chunk = count * modes // chips
    owned = block // energies
    scalars = (energy_weights, collector_low, collector_high)

    pieces, scale, front = call_prepare(
        scalars, inverse_blocks, source, left_coupling, right_coupling, chips
    )
    mine = lax.all_to_all(pieces, "chip", 0, 0, tiled=True)
    given = lax.all_gather(mine, "core")
    out = call_sweeps(given, chunk)
    out = lax.all_to_all(out, "chip", 0, 0, tiled=True)
    out = call_finish(
        scale,
        front,
        inverse_blocks,
        source,
        out.reshape(count, modes, 4 * edge),
        energies,
        owned,
    )
    out = lax.all_to_all(out, "energy", 0, 0, tiled=True)
    return jnp.sum(out.astype(F32), axis=0)[None]


def solution(mesh):
    energies, strips = mesh.devices.shape
    cores = 2
    split = jax.sharding.Mesh(
        mesh.devices.reshape(energies, strips // cores, cores), ("energy", "chip", "core")
    )
    width = ("chip", "core")
    placed = (
        P("energy", width, None),
        P("energy", width, None),
        P(width, None),
        P(width, None),
        P("energy"),
        P(width),
        P(width),
    )
    return jax.shard_map(
        body, mesh=split, in_specs=placed, out_specs=P(width, "energy", None), check_vma=False
    )
```
